32 devices in a mesh: ctx: 4 (over z), ch: 8 (over y, x, core).
Axes of the slice: x: 2, y: 2, z: 4, core: 2. Of those that a mesh axis runs over, the one named last changes fastest.
Arguments:
- stream: bfloat16 [512, 8192], P('ctx', 'ch'), may hold values from -6 to 6
- in_weight: bfloat16 [8192, 3, 8192], P(None, None, 'ch'), may hold values from -0.0625 to 0.0625
- pole_rate: float32 [8192, 16], P('ch'), may hold values from 0.0009765625 to 0.05
- residue: float32 [8192, 16], P('ch'), may hold values from -1.5 to 1.5
- skip_gain: float32 [8192], P('ch'), may hold values from -4 to 4
- doc_lengths: int32 [8], replicated, may hold values from 1 to 256, 512 in all
Outputs:
- mixed: bfloat16 [512, 8192], P('ctx', 'ch')
The draws below stay inside these ranges and needn't reach their ends.
Inputs may be any that keep to these rules, and one draw needn't show every extreme that they name: `doc_lengths`: the 8 documents lie end to end and cover the row: the lengths sum to 512, and the longest has exactly 512 // 2 tokens.
All inputs are finite; a program needn't handle non-finite values.
Results may differ from the reference program's by a relative error of at most 0.003.
Values may be sent and summed in bfloat16 or wider, within the bound.
No kernel may reach another device: no remote copies, remote signals or barrier semaphores. Data moves between devices by JAX's collectives and lax.ppermute only.
A program may use at most 192 MiB of HBM per device.

```python
import math
import jax
import jax.numpy as jnp
import numpy as np
from jax import lax

D = 8192
MODES = 16
DOCS = 8
TOKENS = 512


def levels(stream_key, extent, cuts, least, high):
    def one(axis_at, shards_of):
        draws = jax.random.uniform(jax.random.fold_in(jax.random.fold_in(stream_key, 6), axis_at), (shards_of,), jnp.float32, least / len(cuts), high / len(cuts))
        return jnp.repeat(jnp.exp(draws), extent[axis_at] // shards_of).reshape((-1,) + (1,) * (len(extent) - axis_at - 1))

    loudness = one(*cuts[0])
    for cut in cuts[1:]:
        loudness = loudness * one(*cut)
    return loudness


def profile(count, total, reach, slope):
    portions = [(1 << 20) // math.isqrt(rank ** slope) + 1 for rank in range(2, count + 1)]
    rest, counts = total - reach - (count - 1), [1] * (count - 1)
    while rest > 0:
        movable = [i for i in range(count - 1) if counts[i] < reach]
        mass, budget = sum([portions[i] for i in movable]), rest
        for i in movable:
            more = min(reach - counts[i], max(1, budget * portions[i] // mass), rest)
            counts[i] = counts[i] + more
            rest = rest - more
    return np.array([reach] + counts)


def uneven_parts(rng, number_of, total, most, lean):
    if number_of == 2:
        one = jax.random.randint(rng, (), max(1, total - most), min(most, total - 1) + 1)
        return jnp.stack([one, total - one])
    sizes = jnp.asarray(profile(number_of, total, most, lean), jnp.int32)
    pairs = (number_of - 1) // 2
    giver, taker = sizes[1:1 + 2 * pairs:2], sizes[2:2 + 2 * pairs:2]
    margin = jnp.minimum(giver - 1, most - taker)
    shifted = jax.random.randint(jax.random.fold_in(rng, 1), (pairs,), 0, 1 << 20) % (margin + 1)
    sizes = sizes.at[1:1 + 2 * pairs:2].set(giver - shifted).at[2:2 + 2 * pairs:2].set(taker + shifted)
    return sizes[jax.random.permutation(jax.random.fold_in(rng, 2), number_of)]


def normal_values(own_key, extent, deviation, most, split=(), kind=jnp.bfloat16):
    level = levels(own_key, extent, split, -0.22, 0.18) if split else 1.0
    array = jax.random.normal(own_key, extent, jnp.float32) * deviation * level
    return jnp.minimum(jnp.maximum(array, -most), most).astype(kind)


def setup_inputs(seed: int = 0) -> dict:
    key_list = jax.random.split(jax.random.key(seed), 7)
    stream = normal_values(key_list[0], (TOKENS, D), 1.0, 6.0, ((0, 4), (1, 8)))
    in_weight = normal_values(key_list[1], (D, 3, D), D ** -0.5, 0.0625, ((2, 8),))
    pole_rate = jnp.clip(jnp.exp(math.log(0.05) - 3.9357395 * jax.random.uniform(key_list[2], (D, MODES), jnp.float32) ** levels(key_list[2], (D, MODES), ((0, 8),), -0.2, 0.2)), 0.0009765625, 0.05)
    residue = normal_values(key_list[3], (D, MODES), MODES ** -0.5, 1.5, ((0, 8),), jnp.float32)
    skip_gain = normal_values(key_list[4], (D,), 1.0, 4.0, ((0, 8),), jnp.float32)
    doc_lengths = uneven_parts(key_list[5], DOCS, TOKENS, TOKENS // 2, 2).astype(jnp.int32)
    return {"stream": stream, "in_weight": in_weight, "pole_rate": pole_rate, "residue": residue, "skip_gain": skip_gain, "doc_lengths": doc_lengths}


def reference(stream, in_weight, pole_rate, residue, skip_gain, doc_lengths):
    floats = stream.astype(jnp.float32)
    rowscale = lax.rsqrt(lax.optimization_barrier(jnp.sum(floats * floats, axis=1)) / D + 1e-06)
    proj = jnp.dot(stream, in_weight.reshape(D, 3 * D), preferred_element_type=jnp.float32)
    proj = proj * rowscale[:, None]
    outer = proj[:, :D]
    inner = proj[:, D:2 * D]
    values = proj[:, 2 * D:]
    driven = inner * values
    lam = jnp.exp(-pole_rate)
    mix = residue * jnp.sqrt(-jnp.expm1(-2.0 * pole_rate))
    starts = (jnp.cumsum(doc_lengths) - doc_lengths).astype(jnp.int32)
    position = jnp.arange(TOKENS, dtype=jnp.int32)
    is_start = jnp.any(position[:, None] == starts[None, :], axis=1)
    keep = jnp.where(is_start, 0.0, 1.0).astype(jnp.float32)

    def advance(state, inputs):
        drive_row, keep_row = inputs
        state = lam * state * keep_row + drive_row[:, None]
        return (state, lax.optimization_barrier(jnp.sum(mix * state, axis=1)))
    start_state = jnp.zeros((D, MODES), jnp.float32)
    _, filtered = lax.scan(advance, start_state, (driven, keep))
    return (outer * (filtered + skip_gain[None, :] * driven)).astype(jnp.bfloat16)
```

```python
import functools

import jax
import jax.numpy as jnp
from jax import lax
from jax.experimental import pallas as pl
from jax.experimental.pallas import tpu as pltpu
from jax.sharding import PartitionSpec as P

SUB = 8
LANE = 128
IN_VMEM = pl.BlockSpec(memory_space=pltpu.VMEM)
IN_SMEM = pl.BlockSpec(memory_space=pltpu.SMEM)
IN_HBM = pl.BlockSpec(memory_space=pl.ANY)


def shifted(block, axis, distance):
    devices = range(lax.axis_size(axis))
    route = [(i - distance, i) for i in devices if i - distance in devices]
    return lax.ppermute(block, axis, route)


def combine(earlier, later):
    return (earlier[0] * later[0], later[0] * earlier[1] + later[1])


def split_proj(product, squares, width, local):
    rowscale = lax.rsqrt(squares / width + 1e-06)
    proj = product * rowscale[:, None]
    outer = proj[:, :local]
    driven = proj[:, local : 2 * local] * proj[:, 2 * local :]
    return (outer, driven)


def local_scan(driven, keep, lam):
    modes, local = lam.shape
    decay = keep[:, None, None] * lam[None, :, :]
    drive = jnp.broadcast_to(driven[:, None, :], (driven.shape[0], modes, local))
    return lax.associative_scan(combine, (decay, drive), axis=0)


def general(stream, in_weight, pole_rate, residue, skip_gain, doc_lengths):
    rows = stream.shape[0]
    width = in_weight.shape[0]
    local = in_weight.shape[2]
    modes = pole_rate.shape[1]
    weights = in_weight.reshape(width, 3 * local)
    lam = jnp.exp(-pole_rate).T
    mix = (residue * jnp.sqrt(-jnp.expm1(-2.0 * pole_rate))).T
    starts = jnp.cumsum(doc_lengths) - doc_lengths
    position = lax.axis_index("ctx") * rows + jnp.arange(rows, dtype=jnp.int32)
    is_start = jnp.any(position[:, None] == starts[None, :], axis=1)
    keep = jnp.where(is_start, 0.0, 1.0).astype(jnp.float32)
    whole = lax.all_gather(stream, "ch", axis=1, tiled=True)
    floats = whole.astype(jnp.float32)
    squares = jnp.sum(floats * floats, axis=1)
    product = jnp.dot(whole, weights, preferred_element_type=jnp.float32)
    outer, driven = split_proj(product, squares, width, local)
    decay_cum, local_state = local_scan(driven, keep, lam)
    block_decay = decay_cum[-1]
    block_state = local_state[-1]
    zeros_state = jnp.zeros((modes, local), jnp.float32)

    def forward(step, incoming):
        outgoing = block_decay * incoming + block_state
        return shifted(outgoing, "ctx", 1)

    incoming = lax.fori_loop(0, lax.axis_size("ctx") - 1, forward, zeros_state)
    state = local_state + decay_cum * incoming[None, :, :]
    filtered = jnp.einsum("tnc,nc->tc", state, mix)
    return (outer * (filtered + skip_gain[None, :] * driven)).astype(jnp.bfloat16)


def chunk_rows(mask, depth):
    return pl.ds(pl.multiple_of((lax.axis_index("ch") ^ mask) * depth, depth), depth)


def add_squares(sq, blocks):
    total = sq
    for ref in blocks:
        for g in range(ref.shape[1] // LANE):
            v = ref[:, g * LANE : (g + 1) * LANE].astype(jnp.float32)
            total = total + v * v
    return total


def run_copies(copies, ahead):
    for c in copies[:ahead]:
        c.start()

    def wait(i):
        copies[i].wait()
        if i + ahead < len(copies):
            copies[i + ahead].start()

    return wait


def by_groups(value, store):
    for g in range(SUB):
        store(g, value[:, g * LANE : (g + 1) * LANE])


def first_kernel(o, s, wt, rate, res, acc, sq, lam3, mix3, wbuf, xcat, sem):
    depth = o.shape[1]
    copies = [
        pltpu.make_async_copy(
            wt.at[p, chunk_rows(m, depth)], wbuf.at[p, pl.ds(i * depth, depth)], sem.at[2 * p + i]
        )
        for p in range(3)
        for i, m in enumerate((0, 1))
    ]
    wait = run_copies(copies, 4)
    xcat[:, :depth] = o[...]
    xcat[:, depth:] = s[...]
    sq[...] = add_squares(jnp.zeros(sq.shape, jnp.float32), (o, s))
    rates = rate[...]
    lam = jnp.exp(-rates)
    tanh = jnp.tanh(rates)
    mix = res[...] * jnp.sqrt(2.0 * tanh / (1.0 + tanh))

    def put_lam(g, v):
        lam3[:, g, :] = v

    def put_mix(g, v):
        mix3[:, g, :] = v

    by_groups(lam, put_lam)
    by_groups(mix, put_mix)
    for p in range(3):
        wait(2 * p)
        wait(2 * p + 1)
        acc[p] = jnp.dot(xcat[...], wbuf[p], preferred_element_type=jnp.float32)


def second_kernel(x, xs, wt, acc_in, sq_in, acc, sq, cache, wbuf, xcat, sem):
    depth = x.shape[1]
    copies = [
        pltpu.make_async_copy(
            wt.at[p, chunk_rows(m, depth)], wbuf.at[p, pl.ds(i * depth, depth)], sem.at[2 * p + i]
        )
        for p in range(3)
        for i, m in enumerate((2, 3))
    ]
    copies += [
        pltpu.make_async_copy(
            wt.at[1 + p, chunk_rows(m, depth)],
            cache.at[p, pl.ds(i * depth, depth)],
            sem.at[6 + 4 * p + i],
        )
        for p in range(2)
        for i, m in enumerate((4, 6, 5, 7))
    ]
    wait = run_copies(copies, 4)
    xcat[:, :depth] = x[...]
    xcat[:, depth:] = xs[...]
    sq[...] = add_squares(sq_in[...], (x, xs))
    for p in range(3):
        wait(2 * p)
        wait(2 * p + 1)
        acc[p] = acc_in[p] + jnp.dot(xcat[...], wbuf[p], preferred_element_type=jnp.float32)
    for i in range(6, 14):
        wait(i)


def third_kernel(
    y, d, ys, ds, acc_in, sq_in, cache, lam3, docs, xcat, scale, d3, e3
):
    depth = y.shape[1]
    rows = y.shape[0]
    for i, ref in enumerate((y, d, ys, ds)):
        xcat[:, i * depth : (i + 1) * depth] = ref[...]
    total = jnp.sum(add_squares(sq_in[...], (y, d, ys, ds)), axis=1, keepdims=True)
    row = lax.rsqrt(total / (8 * depth) + 1e-06)
    scale[...] = jnp.broadcast_to(row, scale.shape)
    inner = acc_in[1] + jnp.dot(xcat[...], cache[0], preferred_element_type=jnp.float32)
    values = acc_in[2] + jnp.dot(xcat[...], cache[1], preferred_element_type=jnp.float32)
    driven = (inner * row) * (values * row)

    def put(g, v):
        d3[:, g, :] = v

    by_groups(driven, put)
    _, last, _ = own_starts(docs, rows)
    modes = lam3.shape[0]

    def body(step, state):
        for j in range(SUB):
            t = step * SUB + j
            drive = jnp.where(t >= last, d3[t], 0.0)
            state = [lam3[n] * state[n] + drive for n in range(modes)]
        return state

    zeros = [jnp.zeros((SUB, LANE), jnp.float32) for _ in range(modes)]
    state = lax.fori_loop(jnp.maximum(last, 0) // SUB, rows // SUB, body, zeros)
    for n in range(modes):
        e3[n] = state[n]


def own_starts(docs, rows):
    at = -lax.axis_index("ctx") * rows
    first, last, starts = rows, -1, []
    for i in range(docs.shape[0]):
        inside = jnp.logical_and(at >= 0, at < rows)
        first = jnp.where(jnp.logical_and(inside, at < first), at, first)
        last = jnp.where(jnp.logical_and(inside, at > last), at, last)
        starts.append(at)
        at = at + docs[i]
    return first, last, starts


def outer_kernel(xcat, wt, acc_in, d3, lam3, mix3, skip, docs, outer, f3, wbuf, sem):
    rows = xcat.shape[0]
    depth = xcat.shape[1] // 4
    modes = lam3.shape[0]
    copies = [
        pltpu.make_async_copy(
            wt.at[0, chunk_rows(m, depth)], wbuf.at[pl.ds(i * depth, depth)], sem.at[i]
        )
        for i, m in enumerate((4, 6, 5, 7))
    ]
    wait = run_copies(copies, 4)
    _, _, starts = own_starts(docs, rows)

    def body(step, state):
        for j in range(SUB):
            t = step * SUB + j
            begins = starts[0] == t
            for at in starts[1:]:
                begins = jnp.logical_or(begins, at == t)
            keep = jnp.where(begins, 0.0, 1.0)
            drive = d3[t]
            state = [lam3[n] * (state[n] * keep) + drive for n in range(modes)]
            terms = [mix3[n] * state[n] for n in range(modes)]
            while len(terms) > 1:
                terms = [a + b for a, b in zip(terms[::2], terms[1::2])]
            f3[t] = terms[0] + skip[...] * drive
        return state

    zeros = [jnp.zeros((SUB, LANE), jnp.float32) for _ in range(modes)]
    lax.fori_loop(0, rows // SUB, body, zeros)
    for i in range(4):
        wait(i)
    outer[...] = acc_in[0] + jnp.dot(xcat[...], wbuf[...], preferred_element_type=jnp.float32)


def last_kernel(*refs, count):
    arrived = refs[:count]
    outer, f3, scale, lam3, mix3, docs, out = refs[count:]
    rows = outer.shape[0]
    modes = lam3.shape[0]
    first, _, starts = own_starts(docs, rows)
    me = lax.axis_index("ctx")
    begins, valid = [], None
    for k in range(1, count + 1):
        if k > 1:
            inside = [jnp.logical_and(at >= -(k - 1) * rows, at < -(k - 2) * rows) for at in starts]
            clear = jnp.logical_not(functools.reduce(jnp.logical_or, inside))
            valid = jnp.logical_and(jnp.logical_and(valid, clear), me >= k)
        else:
            valid = me >= 1
        begins.append(valid)
    state = []
    for n in range(modes):
        lam = lam3[n]
        whole = lam
        for _ in range(rows.bit_length() - 1):
            whole = whole * whole
        power, total = 1.0, jnp.zeros((SUB, LANE), jnp.float32)
        for k in range(count):
            total = total + jnp.where(begins[k], power * arrived[k][n], 0.0)
            power = power * whole
        state.append(mix3[n] * total)

    def body(step, state):
        for j in range(SUB):
            t = step * SUB + j
            state = [lam3[n] * state[n] for n in range(modes)]
            terms = list(state)
            while len(terms) > 1:
                terms = [a + b for a, b in zip(terms[::2], terms[1::2])]
            f3[t] = f3[t] + jnp.where(t < first, terms[0], 0.0)
        return state

    lax.fori_loop(0, (first + SUB - 1) // SUB, body, state)
    for g in range(SUB):
        cols = slice(g * LANE, (g + 1) * LANE)
        out[:, cols] = (outer[:, cols] * scale[...] * f3[:, g, :]).astype(out.dtype)


def params(mib):
    return pltpu.CompilerParams(vmem_limit_bytes=mib << 20)


def fitted(stream, in_weight, pole_rate, residue, skip_gain, doc_lengths, reach):
    rows, depth = stream.shape
    width, _, local = in_weight.shape
    modes = pole_rate.shape[1]
    size = lax.axis_size("ch")
    wt = jnp.transpose(in_weight, (1, 0, 2))
    rate, res = pole_rate.T, residue.T
    f32, b16 = jnp.float32, jnp.bfloat16
    dma = pltpu.SemaphoreType.DMA

    def swap(block, mask):
        return lax.ppermute(block, "ch", [(i, i ^ mask) for i in range(size)])

    s, x, y, d = (swap(stream, m) for m in (1, 2, 4, 6))
    planes = pltpu.VMEM((3, rows, local), f32)
    squares = pltpu.VMEM((rows, LANE), f32)
    poles = pltpu.VMEM((modes, SUB, LANE), f32)
    cost = functools.partial(pl.CostEstimate, transcendentals=0)
    acc, sq, lam3, mix3 = pl.pallas_call(
        first_kernel,
        in_specs=[IN_VMEM, IN_VMEM, IN_HBM, IN_VMEM, IN_VMEM],
        out_specs=[IN_VMEM] * 4,
        out_shape=[planes, squares, poles, poles],
        scratch_shapes=[
            pltpu.VMEM((3, 2 * depth, local), b16),
            pltpu.VMEM((rows, 2 * depth), b16),
            dma((6,)),
        ],
        compiler_params=params(18),
        cost_estimate=cost(flops=12 * rows * depth * local, bytes_accessed=12 * depth * local),
        name="first",
    )(stream, s, wt, rate, res)
    xs = swap(x, 1)
    acc, sq, cache = pl.pallas_call(
        second_kernel,
        in_specs=[IN_VMEM, IN_VMEM, IN_HBM, IN_VMEM, IN_VMEM],
        out_specs=[IN_VMEM] * 3,
        out_shape=[planes, squares, pltpu.VMEM((2, 4 * depth, local), b16)],
        scratch_shapes=[
            pltpu.VMEM((3, 2 * depth, local), b16),
            pltpu.VMEM((rows, 2 * depth), b16),
            dma((14,)),
        ],
        compiler_params=params(18),
        cost_estimate=cost(flops=12 * rows * depth * local, bytes_accessed=28 * depth * local),
        name="second",
    )(x, xs, wt, acc, sq)
    ys, ds = swap(y, 1), swap(d, 1)
    tokens = pltpu.VMEM((rows, SUB, LANE), f32)
    xcat, scale, d3, e3 = pl.pallas_call(
        third_kernel,
        in_specs=[IN_VMEM] * 8 + [IN_SMEM],
        out_specs=[IN_VMEM] * 4,
        out_shape=[pltpu.VMEM((rows, 4 * depth), b16), squares, tokens, poles],
        compiler_params=params(8),
        cost_estimate=cost(flops=16 * rows * depth * local, bytes_accessed=0),
        name="third",
    )(y, d, ys, ds, acc, sq, cache, lam3, doc_lengths)
    ring = lax.axis_size("ctx")
    arrived = [
        lax.ppermute(e3, "ctx", [(i, (i + k) % ring) for i in range(ring)])
        for k in range(1, reach + 1)
    ]
    outer, f3 = pl.pallas_call(
        outer_kernel,
        in_specs=[IN_VMEM, IN_HBM] + [IN_VMEM] * 5 + [IN_SMEM],
        out_specs=[IN_VMEM] * 2,
        out_shape=[pltpu.VMEM((rows, local), f32), tokens],
        scratch_shapes=[pltpu.VMEM((4 * depth, local), b16), dma((4,))],
        compiler_params=params(14),
        cost_estimate=cost(flops=8 * rows * depth * local, bytes_accessed=8 * depth * local),
        name="outer",
    )(xcat, wt, acc, d3, lam3, mix3, skip_gain.reshape(SUB, LANE), doc_lengths)
    return pl.pallas_call(
        functools.partial(last_kernel, count=reach),
        in_specs=[IN_VMEM] * (reach + 5) + [IN_SMEM],
        out_specs=IN_VMEM,
        out_shape=jax.ShapeDtypeStruct((rows, local), b16),
        compiler_params=params(8),
        name="last",
    )(*arrived, outer, f3, scale, lam3, mix3, doc_lengths)


def solution(mesh):
    placed = (P("ctx", "ch"), P(None, None, "ch"), P("ch", None), P("ch", None), P("ch"), P())
    ring = mesh.shape["ctx"]

    def per_device(*args):
        stream, in_weight = args[0], args[1]
        rows, depth = stream.shape
        longest = rows * ring // 2
        reach = min(ring - 1, (longest + rows - 2) // rows)
        if mesh.shape["ch"] == 8 and in_weight.shape[2] == SUB * LANE and rows == LANE:
            return fitted(*args, reach)
        return general(*args)

    return jax.shard_map(
        per_device, mesh=mesh, in_specs=placed, out_specs=P("ctx", "ch"), check_vma=False
    )
```

```python
import functools

import jax
import jax.numpy as jnp
from jax import lax
from jax.experimental import pallas as pl
from jax.experimental.pallas import tpu as pltpu
from jax.sharding import PartitionSpec as P

SUB = 8
LANE = 128
IN_VMEM = pl.BlockSpec(memory_space=pltpu.VMEM)
IN_HBM = pl.BlockSpec(memory_space=pltpu.HBM)
IN_SMEM = pl.BlockSpec(memory_space=pltpu.SMEM)
DRIVEN = (1, 2)
GATE = (0,)


def shifted(block, axis, distance):
    devices = range(lax.axis_size(axis))
    route = [(i - distance, i) for i in devices if i - distance in devices]
    return lax.ppermute(block, axis, route)


def combine(earlier, later):
    return (earlier[0] * later[0], later[0] * earlier[1] + later[1])


def split_proj(product, squares, width, local):
    rowscale = lax.rsqrt(squares / width + 1e-06)
    proj = product * rowscale[:, None]
    outer = proj[:, :local]
    driven = proj[:, local : 2 * local] * proj[:, 2 * local :]
    return (outer, driven)


def local_scan(driven, keep, lam):
    modes, local = lam.shape
    decay = keep[:, None, None] * lam[None, :, :]
    drive = jnp.broadcast_to(driven[:, None, :], (driven.shape[0], modes, local))
    return lax.associative_scan(combine, (decay, drive), axis=0)


def general(stream, in_weight, pole_rate, residue, skip_gain, doc_lengths):
    rows = stream.shape[0]
    width = in_weight.shape[0]
    local = in_weight.shape[2]
    modes = pole_rate.shape[1]
    weights = in_weight.reshape(width, 3 * local)
    lam = jnp.exp(-pole_rate).T
    mix = (residue * jnp.sqrt(-jnp.expm1(-2.0 * pole_rate))).T
    starts = jnp.cumsum(doc_lengths) - doc_lengths
    position = lax.axis_index("ctx") * rows + jnp.arange(rows, dtype=jnp.int32)
    is_start = jnp.any(position[:, None] == starts[None, :], axis=1)
    keep = jnp.where(is_start, 0.0, 1.0).astype(jnp.float32)
    whole = lax.all_gather(stream, "ch", axis=1, tiled=True)
    floats = whole.astype(jnp.float32)
    squares = jnp.sum(floats * floats, axis=1)
    product = jnp.dot(whole, weights, preferred_element_type=jnp.float32)
    outer, driven = split_proj(product, squares, width, local)
    decay_cum, local_state = local_scan(driven, keep, lam)
    block_decay = decay_cum[-1]
    block_state = local_state[-1]
    zeros_state = jnp.zeros((modes, local), jnp.float32)

    def forward(step, incoming):
        outgoing = block_decay * incoming + block_state
        return shifted(outgoing, "ctx", 1)

    incoming = lax.fori_loop(0, lax.axis_size("ctx") - 1, forward, zeros_state)
    state = local_state + decay_cum * incoming[None, :, :]
    filtered = jnp.einsum("tnc,nc->tc", state, mix)
    return (outer * (filtered + skip_gain[None, :] * driven)).astype(jnp.bfloat16)


def chunk_rows(mask, depth):
    return pl.ds(pl.multiple_of((lax.axis_index("ch") ^ mask) * depth, depth), depth)


def add_squares(sq, blocks):
    total = sq
    for ref in blocks:
        for g in range(ref.shape[1] // LANE):
            v = ref[:, g * LANE : (g + 1) * LANE].astype(jnp.float32)
            total = total + v * v
    return total


def by_groups(value, store):
    for g in range(SUB):
        store(g, value[:, g * LANE : (g + 1) * LANE])


def dot(a, b):
    return jnp.dot(a, b, preferred_element_type=jnp.float32)


def run_copies(copies, ahead):
    for c in copies[:ahead]:
        c.start()

    def wait(i):
        copies[i].wait()
        if i + ahead < len(copies):
            copies[i + ahead].start()

    return wait


def weight_copies(wt, planes, masks, depth, target, sem, at=0):
    return [
        pltpu.make_async_copy(
            wt.at[p, chunk_rows(m, depth)],
            target.at[k, pl.ds(i * depth, depth)],
            sem.at[at + k * len(masks) + i],
        )
        for k, p in enumerate(planes)
        for i, m in enumerate(masks)
    ]


def project(blocks, weights, plane):
    depth = blocks[0].shape[1]
    total = dot(blocks[0][...], weights[plane, :depth])
    for i in range(1, len(blocks)):
        total = total + dot(blocks[i][...], weights[plane, i * depth : (i + 1) * depth])
    return total


def own_masks():
    core = lax.axis_index("ch") & 1
    one, two = 2 + 2 * core, 4 - 2 * core
    return (one, two, 6)


def other_masks():
    core = lax.axis_index("ch") & 1
    one, two = 2 + 2 * core, 4 - 2 * core
    return (two ^ 1, one ^ 1, 7)


def first_kernel(
    o, s, wt, rate, res, acc, sq, lam3, mix3, held, near, far, wbuf, rates, ress, sem, small
):
    depth = s.shape[1]
    own = [
        pltpu.make_async_copy(o, held, small.at[0]),
        pltpu.make_async_copy(rate, rates, small.at[1]),
        pltpu.make_async_copy(res, ress, small.at[2]),
    ]
    for c in own:
        c.start()
    copies = weight_copies(wt, DRIVEN, (0, 1), depth, wbuf, sem)
    copies += weight_copies(wt, DRIVEN, own_masks(), depth, near, sem, 4)
    copies += weight_copies(wt, DRIVEN, other_masks(), depth, far, sem, 10)
    wait = run_copies(copies, 8)
    for c in own:
        c.wait()
    blocks = (held, s)
    sq[...] = add_squares(jnp.zeros(sq.shape, jnp.float32), blocks)
    r = rates[...]
    lam = jnp.exp(-r)
    tanh = jnp.tanh(r)
    mix = ress[...] * jnp.sqrt(2.0 * tanh / (1.0 + tanh))

    def put_lam(g, v):
        lam3[:, g, :] = v

    def put_mix(g, v):
        mix3[:, g, :] = v

    by_groups(lam, put_lam)
    by_groups(mix, put_mix)
    for k in range(2):
        wait(2 * k)
        wait(2 * k + 1)
        acc[k] = project(blocks, wbuf, k)
    for i in range(4, len(copies)):
        wait(i)


def near_kernel(a, b, d, weights, acc_in, sq_in, acc, sq):
    blocks = (a, b, d)
    sq[...] = add_squares(sq_in[...], blocks)
    for k in range(2):
        acc[k] = acc_in[k] + project(blocks, weights, k)


def far_kernel(a, b, d, weights, wt, acc_in, sq_in, lam3, docs, scale, d3, e3, gate, sem):
    rows, depth = a.shape
    wait = run_copies(weight_copies(wt, GATE, (0, 1), depth, gate, sem), 8)
    blocks = (a, b, d)
    total = jnp.sum(add_squares(sq_in[...], blocks), axis=1, keepdims=True)
    row = lax.rsqrt(total / (8 * depth) + 1e-06)
    scale[...] = jnp.broadcast_to(row, scale.shape)
    inner = acc_in[0] + project(blocks, weights, 0)
    values = acc_in[1] + project(blocks, weights, 1)
    driven = (inner * row) * (values * row)

    def put(g, v):
        d3[:, g, :] = v

    by_groups(driven, put)
    _, last, _ = own_starts(docs, rows)
    modes = lam3.shape[0]

    def body(step, state):
        for j in range(SUB):
            t = step * SUB + j
            drive = jnp.where(t >= last, d3[t], 0.0)
            state = [lam3[n] * state[n] + drive for n in range(modes)]
        return state

    zeros = [jnp.zeros((SUB, LANE), jnp.float32) for _ in range(modes)]
    state = lax.fori_loop(jnp.maximum(last, 0) // SUB, rows // SUB, body, zeros)
    for n in range(modes):
        e3[n] = state[n]
    for i in range(2):
        wait(i)


def own_starts(docs, rows):
    at = -lax.axis_index("ctx") * rows
    first, last, starts = rows, -1, []
    for i in range(docs.shape[0]):
        inside = jnp.logical_and(at >= 0, at < rows)
        first = jnp.where(jnp.logical_and(inside, at < first), at, first)
        last = jnp.where(jnp.logical_and(inside, at > last), at, last)
        starts.append(at)
        at = at + docs[i]
    return first, last, starts


def outer_kernel(
    o, s, a, b, d, ao, bo, do, wt, gate, d3, lam3, mix3, skip, docs, outer, f3, wbuf, sem
):
    rows, depth = o.shape
    masks = own_masks() + other_masks()
    wait = run_copies(weight_copies(wt, GATE, masks, depth, wbuf, sem), 8)
    modes = lam3.shape[0]
    _, _, starts = own_starts(docs, rows)

    def body(step, state):
        for j in range(SUB):
            t = step * SUB + j
            begins = starts[0] == t
            for at in starts[1:]:
                begins = jnp.logical_or(begins, at == t)
            keep = jnp.where(begins, 0.0, 1.0)
            drive = d3[t]
            state = [lam3[n] * (state[n] * keep) + drive for n in range(modes)]
            terms = [mix3[n] * state[n] for n in range(modes)]
            while len(terms) > 1:
                terms = [p + q for p, q in zip(terms[::2], terms[1::2])]
            f3[t] = terms[0] + skip[...] * drive
        return state

    zeros = [jnp.zeros((SUB, LANE), jnp.float32) for _ in range(modes)]
    lax.fori_loop(0, rows // SUB, body, zeros)
    total = project((o, s), gate, 0)
    for i, block in enumerate((a, b, d, ao, bo, do)):
        wait(i)
        total = total + dot(block[...], wbuf[0, i * depth : (i + 1) * depth])
    outer[...] = total


def last_kernel(*refs, count):
    arrived = refs[:count]
    outer, f3, scale, lam3, mix3, docs, out = refs[count:]
    rows = outer.shape[0]
    modes = lam3.shape[0]
    first, _, starts = own_starts(docs, rows)
    me = lax.axis_index("ctx")
    begins, valid = [], None
    for k in range(1, count + 1):
        if k > 1:
            inside = [jnp.logical_and(at >= -(k - 1) * rows, at < -(k - 2) * rows) for at in starts]
            clear = jnp.logical_not(functools.reduce(jnp.logical_or, inside))
            valid = jnp.logical_and(jnp.logical_and(valid, clear), me >= k)
        else:
            valid = me >= 1
        begins.append(valid)
    state = []
    for n in range(modes):
        lam = lam3[n]
        whole = lam
        for _ in range(rows.bit_length() - 1):
            whole = whole * whole
        power, total = 1.0, jnp.zeros((SUB, LANE), jnp.float32)
        for k in range(count):
            total = total + jnp.where(begins[k], power * arrived[k][n], 0.0)
            power = power * whole
        state.append(mix3[n] * total)

    def body(step, state):
        for j in range(SUB):
            t = step * SUB + j
            state = [lam3[n] * state[n] for n in range(modes)]
            terms = list(state)
            while len(terms) > 1:
                terms = [a + b for a, b in zip(terms[::2], terms[1::2])]
            f3[t] = f3[t] + jnp.where(t < first, terms[0], 0.0)
        return state

    lax.fori_loop(0, (first + SUB - 1) // SUB, body, state)
    for g in range(SUB):
        cols = slice(g * LANE, (g + 1) * LANE)
        out[:, cols] = (outer[:, cols] * scale[...] * f3[:, g, :]).astype(out.dtype)


def params(mib):
    return pltpu.CompilerParams(vmem_limit_bytes=mib << 20)


def fitted(stream, in_weight, pole_rate, residue, skip_gain, doc_lengths, reach):
    rows, depth = stream.shape
    width, _, local = in_weight.shape
    modes = pole_rate.shape[1]
    size = lax.axis_size("ch")
    wt = jnp.transpose(in_weight, (1, 0, 2))
    rate, res = pole_rate.T, residue.T
    f32, b16 = jnp.float32, jnp.bfloat16
    dma = pltpu.SemaphoreType.DMA

    def swap(block, mask):
        return lax.ppermute(block, "ch", [(i, i ^ mask) for i in range(size)])

    def split(block, first):
        masks = (2, 4) if first else (4, 2)
        return lax.ppermute(block, "ch", [(i, i ^ masks[i & 1]) for i in range(size)])

    def call(kernel, ins, outs, scratch, flops, mib):
        return pl.pallas_call(
            kernel,
            in_specs=[spec for spec, _ in ins],
            out_specs=[IN_VMEM] * len(outs),
            out_shape=outs,
            scratch_shapes=scratch,
            compiler_params=params(mib),
            cost_estimate=pl.CostEstimate(
                flops=2 * rows * depth * local * flops, bytes_accessed=0, transcendentals=0
            ),
            name=kernel.__name__,
        )(*[array for _, array in ins])

    def here(*arrays):
        return [(IN_VMEM, a) for a in arrays]

    planes = pltpu.VMEM((2, rows, local), f32)
    squares = pltpu.VMEM((rows, LANE), f32)
    poles = pltpu.VMEM((modes, SUB, LANE), f32)
    tokens = pltpu.VMEM((rows, SUB, LANE), f32)
    chunk = pltpu.VMEM((rows, depth), b16)
    vector = pltpu.VMEM((modes, local), f32)

    def there(*arrays):
        return [(IN_HBM, pltpu.with_memory_space_constraint(a, pltpu.HBM)) for a in arrays]

    def weights(planes_of, chunks):
        return pltpu.VMEM((planes_of, chunks * depth, local), b16)

    s = swap(stream, 1)
    a, b, d = split(stream, True), split(stream, False), swap(stream, 6)
    acc, sq, lam3, mix3, o, near, far = call(
        first_kernel,
        there(stream) + here(s) + there(wt, rate, res),
        [planes, squares, poles, poles, chunk, weights(2, 3), weights(2, 3)],
        [weights(2, 2), vector, vector, dma((16,)), dma((3,))],
        4,
        12,
    )
    a, b, d, acc, sq = lax.optimization_barrier((a, b, d, acc, sq))
    ao, bo, do = swap(a, 1), swap(b, 1), swap(d, 1)
    acc, sq = call(near_kernel, here(a, b, d, near, acc, sq), [planes, squares], [], 6, 4)
    scale, d3, e3, gate = call(
        far_kernel,
        here(ao, bo, do, far) + there(wt) + here(acc, sq, lam3) + [(IN_SMEM, doc_lengths)],
        [squares, tokens, poles, weights(1, 2)],
        [dma((2,))],
        6,
        4,
    )
    ring = lax.axis_size("ctx")
    arrived = [
        lax.ppermute(e3, "ctx", [(i, (i + k) % ring) for i in range(ring)])
        for k in range(1, reach + 1)
    ]
    outer, f3 = call(
        outer_kernel,
        here(o, s, a, b, d, ao, bo, do)
        + there(wt)
        + here(gate, d3, lam3, mix3, skip_gain.reshape(SUB, LANE))
        + [(IN_SMEM, doc_lengths)],
        [pltpu.VMEM((rows, local), f32), tokens],
        [weights(1, 6), dma((6,))],
        8,
        16,
    )
    return pl.pallas_call(
        functools.partial(last_kernel, count=reach),
        in_specs=[IN_VMEM] * (reach + 5) + [IN_SMEM],
        out_specs=IN_VMEM,
        out_shape=jax.ShapeDtypeStruct((rows, local), b16),
        compiler_params=params(8),
        name="last",
    )(*arrived, outer, f3, scale, lam3, mix3, doc_lengths)


def solution(mesh):
    placed = (P("ctx", "ch"), P(None, None, "ch"), P("ch", None), P("ch", None), P("ch"), P())
    ring = mesh.shape["ctx"]

    def per_device(*args):
        stream, in_weight = args[0], args[1]
        rows, depth = stream.shape
        longest = rows * ring // 2
        reach = min(ring - 1, (longest + rows - 2) // rows)
        if mesh.shape["ch"] == 8 and in_weight.shape[2] == SUB * LANE and rows == LANE:
            return fitted(*args, reach)
        return general(*args)

    return jax.shard_map(
        per_device, mesh=mesh, in_specs=placed, out_specs=P("ctx", "ch"), check_vma=False
    )
```

```python
import functools

import jax
import jax.numpy as jnp
from jax import lax
from jax.experimental import pallas as pl
from jax.experimental.pallas import tpu as pltpu
from jax.sharding import PartitionSpec as P

SUB = 8
LANE = 128
IN_VMEM = pl.BlockSpec(memory_space=pltpu.VMEM)
IN_HBM = pl.BlockSpec(memory_space=pltpu.HBM)
DRIVEN = (1, 2)
GATE = (0,)


def shifted(block, axis, distance):
    devices = range(lax.axis_size(axis))
    route = [(i - distance, i) for i in devices if i - distance in devices]
    return lax.ppermute(block, axis, route)


def combine(earlier, later):
    return (earlier[0] * later[0], later[0] * earlier[1] + later[1])


def split_proj(product, squares, width, local):
    rowscale = lax.rsqrt(squares / width + 1e-06)
    proj = product * rowscale[:, None]
    outer = proj[:, :local]
    driven = proj[:, local : 2 * local] * proj[:, 2 * local :]
    return (outer, driven)


def local_scan(driven, keep, lam):
    modes, local = lam.shape
    decay = keep[:, None, None] * lam[None, :, :]
    drive = jnp.broadcast_to(driven[:, None, :], (driven.shape[0], modes, local))
    return lax.associative_scan(combine, (decay, drive), axis=0)


def general(stream, in_weight, pole_rate, residue, skip_gain, doc_lengths):
    rows = stream.shape[0]
    width = in_weight.shape[0]
    local = in_weight.shape[2]
    modes = pole_rate.shape[1]
    weights = in_weight.reshape(width, 3 * local)
    lam = jnp.exp(-pole_rate).T
    mix = (residue * jnp.sqrt(-jnp.expm1(-2.0 * pole_rate))).T
    starts = jnp.cumsum(doc_lengths) - doc_lengths
    position = lax.axis_index("ctx") * rows + jnp.arange(rows, dtype=jnp.int32)
    is_start = jnp.any(position[:, None] == starts[None, :], axis=1)
    keep = jnp.where(is_start, 0.0, 1.0).astype(jnp.float32)
    whole = lax.all_gather(stream, "ch", axis=1, tiled=True)
    floats = whole.astype(jnp.float32)
    squares = jnp.sum(floats * floats, axis=1)
    product = jnp.dot(whole, weights, preferred_element_type=jnp.float32)
    outer, driven = split_proj(product, squares, width, local)
    decay_cum, local_state = local_scan(driven, keep, lam)
    block_decay = decay_cum[-1]
    block_state = local_state[-1]
    zeros_state = jnp.zeros((modes, local), jnp.float32)

    def forward(step, incoming):
        outgoing = block_decay * incoming + block_state
        return shifted(outgoing, "ctx", 1)

    incoming = lax.fori_loop(0, lax.axis_size("ctx") - 1, forward, zeros_state)
    state = local_state + decay_cum * incoming[None, :, :]
    filtered = jnp.einsum("tnc,nc->tc", state, mix)
    return (outer * (filtered + skip_gain[None, :] * driven)).astype(jnp.bfloat16)


def chunk_rows(mask, depth):
    return pl.ds(pl.multiple_of((lax.axis_index("ch") ^ mask) * depth, depth), depth)


def add_squares(sq, blocks):
    total = sq
    for ref in blocks:
        for g in range(ref.shape[1] // LANE):
            v = ref[:, g * LANE : (g + 1) * LANE].astype(jnp.float32)
            total = total + v * v
    return total


def by_groups(value, store):
    for g in range(SUB):
        store(g, value[:, g * LANE : (g + 1) * LANE])


def dot(a, b):
    return jnp.dot(a, b, preferred_element_type=jnp.float32)


def run_copies(copies, ahead):
    for c in copies[:ahead]:
        c.start()

    def wait(i):
        copies[i].wait()
        if i + ahead < len(copies):
            copies[i + ahead].start()

    return wait


def weight_copies(wt, planes, masks, depth, target, sem, at=0):
    return [
        pltpu.make_async_copy(
            wt.at[p, chunk_rows(m, depth)],
            target.at[k, pl.ds(i * depth, depth)],
            sem.at[at + k * len(masks) + i],
        )
        for k, p in enumerate(planes)
        for i, m in enumerate(masks)
    ]


def project(blocks, weights, plane):
    depth = blocks[0].shape[1]
    total = dot(blocks[0][...], weights[plane, :depth])
    for i in range(1, len(blocks)):
        total = total + dot(blocks[i][...], weights[plane, i * depth : (i + 1) * depth])
    return total


def own_masks():
    core = lax.axis_index("ch") & 1
    one, two = 2 + 2 * core, 4 - 2 * core
    return (one, two, 6)


def other_masks():
    core = lax.axis_index("ch") & 1
    one, two = 2 + 2 * core, 4 - 2 * core
    return (two ^ 1, one ^ 1, 7)


def first_kernel(
    o, s, wt, rate, res, lengths, acc, outer, sq, lam3, mix3, near, far, gate, rowmask, valid, held, wbuf, gbuf, rates, ress, docs, sem, small
):
    rows, depth = s.shape
    own = [
        pltpu.make_async_copy(o, held, small.at[0]),
        pltpu.make_async_copy(rate, rates, small.at[1]),
        pltpu.make_async_copy(res, ress, small.at[2]),
        pltpu.make_async_copy(lengths, docs, small.at[3]),
    ]
    copies = weight_copies(wt, DRIVEN, (0, 1), depth, wbuf, sem)
    copies += weight_copies(wt, GATE, (0, 1), depth, gbuf, sem, 4)
    copies += weight_copies(wt, DRIVEN, own_masks(), depth, near, sem, 6)
    copies += weight_copies(wt, DRIVEN, other_masks()[:2], depth, far, sem, 12)
    copies += weight_copies(wt, GATE, own_masks()[:1], depth, gate, sem, 16)
    run_copies(own, len(own))
    wait = run_copies(copies, 8)
    for c in own:
        c.wait()
    blocks = (held, s)
    sq[...] = add_squares(jnp.zeros(sq.shape, jnp.float32), blocks)
    r = rates[...]
    lam = jnp.exp(-r)
    tanh = jnp.tanh(r)
    mix = ress[...] * jnp.sqrt(2.0 * tanh / (1.0 + tanh))

    def put_lam(g, v):
        lam3[:, g, :] = v

    def put_mix(g, v):
        mix3[:, g, :] = v

    by_groups(lam, put_lam)
    by_groups(mix, put_mix)
    mark_rows(docs, rows, rowmask, valid)
    for k in range(2):
        wait(2 * k)
        wait(2 * k + 1)
        acc[k] = project(blocks, wbuf, k)
    wait(4)
    wait(5)
    outer[...] = project(blocks, gbuf, 0)
    for i in range(6, len(copies)):
        wait(i)


def near_kernel(a, b, d, weights, wt, acc_in, sq_in, acc, sq, far, sem):
    blocks = (a, b, d)
    wait = run_copies(weight_copies(wt, DRIVEN, other_masks()[2:], a.shape[1], far, sem), 8)
    sq[...] = add_squares(sq_in[...], blocks)

    @pl.loop(0, 2)
    def _(k):
        acc[k] = acc_in[k] + project(blocks, weights, k)

    for i in range(2):
        wait(i)


def far_kernel(
    a, b, d, weights, last_weights, wt, acc_in, sq_in, lam3, rowmask, scale, d3, e3, gate, both, sem
):
    rows, depth = a.shape
    wait = run_copies(weight_copies(wt, GATE, own_masks()[1:] + other_masks()[:1], depth, gate, sem), 8)
    blocks = (a, b, d)
    total = jnp.sum(add_squares(sq_in[...], blocks), axis=1, keepdims=True)
    row = lax.rsqrt(total / (8 * depth) + 1e-06)
    scale[...] = jnp.broadcast_to(row, scale.shape)

    @pl.loop(0, 2)
    def _(k):
        both[k] = acc_in[k] + project((a, b), weights, k) + project((d,), last_weights, k)

    for g in range(SUB):
        cols = slice(g * LANE, (g + 1) * LANE)
        d3[:, g, :] = (both[0, :, cols] * scale[...]) * (both[1, :, cols] * scale[...])
    modes = lam3.shape[0]

    def body(step, state):
        first = pl.multiple_of(step * SUB, SUB)
        counts = rowmask[0, pl.ds(first, SUB), :]
        for j in range(SUB):
            drive = d3[first + j] * counts[j : j + 1, :]
            state = [lam3[n] * state[n] + drive for n in range(modes)]
        return state

    zeros = [jnp.zeros((SUB, LANE), jnp.float32) for _ in range(modes)]
    state = lax.fori_loop(0, rows // SUB, body, zeros)
    for n in range(modes):
        e3[n] = state[n]
    for i in range(3):
        wait(i)


def mark_rows(docs, rows, rowmask, valid):
    me = lax.axis_index("ctx")
    at = -me * rows
    first, last, starts = rows, -1, []
    for i in range(docs.shape[0]):
        inside = jnp.logical_and(at >= 0, at < rows)
        first = jnp.where(jnp.logical_and(inside, at < first), at, first)
        last = jnp.where(jnp.logical_and(inside, at > last), at, last)
        starts.append(at)
        at = at + docs[i]
    token = lax.broadcasted_iota(jnp.int32, rowmask.shape[1:], 0)
    rowmask[0] = jnp.where(token >= last, 1.0, 0.0)
    keep = jnp.ones(rowmask.shape[1:], jnp.float32)
    for at in starts:
        keep = jnp.where(token == at, 0.0, keep)
    rowmask[1] = keep
    rowmask[2] = jnp.where(token < first, 1.0, 0.0)
    reached = me >= 1
    for k in range(valid.shape[0]):
        if k > 0:
            for at in starts:
                between = jnp.logical_and(at >= -k * rows, at < -(k - 1) * rows)
                reached = jnp.logical_and(reached, jnp.logical_not(between))
            reached = jnp.logical_and(reached, me >= k + 1)
        valid[k] = jnp.full(valid.shape[1:], jnp.where(reached, 1.0, 0.0))


def outer_kernel(
    a, b, d, ao, bo, do, wt, sum_in, gate_a, gate_far, d3, lam3, mix3, skip, rowmask, outer, f3, wbuf, sem
):
    rows, depth = a.shape
    modes = lam3.shape[0]
    wait = run_copies(weight_copies(wt, GATE, other_masks()[1:], depth, wbuf, sem), 8)

    def body(step, state):
        first = pl.multiple_of(step * SUB, SUB)
        keeps = rowmask[1, pl.ds(first, SUB), :]
        for j in range(SUB):
            drive = d3[first + j]
            state = [lam3[n] * (state[n] * keeps[j : j + 1, :]) + drive for n in range(modes)]
            terms = [mix3[n] * state[n] for n in range(modes)]
            while len(terms) > 1:
                terms = [p + q for p, q in zip(terms[::2], terms[1::2])]
            f3[first + j] = terms[0] + skip[...] * drive
        return state

    zeros = [jnp.zeros((SUB, LANE), jnp.float32) for _ in range(modes)]
    lax.fori_loop(0, rows // SUB, body, zeros)
    total = sum_in[...] + project((a,), gate_a, 0) + project((b, d, ao), gate_far, 0)
    wait(0)
    wait(1)
    outer[...] = total + project((bo, do), wbuf, 0)


def last_kernel(*refs, count):
    arrived = refs[:count]
    outer, f3, scale, lam3, mix3, rowmask, valid, out = refs[count:]
    rows = outer.shape[0]
    modes = lam3.shape[0]
    @pl.when(lax.axis_index("ctx") > 0)
    def _():
        state = []
        for n in range(modes):
            lam = lam3[n]
            whole = lam
            for _ in range(rows.bit_length() - 1):
                whole = whole * whole
            power, total = valid[0], jnp.zeros((SUB, LANE), jnp.float32)
            for k in range(count):
                total = total + power * arrived[k][n]
                if k + 1 < count:
                    power = valid[k + 1] * whole if k == 0 else valid[k + 1] * (power * whole)
            state.append(mix3[n] * total)

        def body(step, state):
            first = pl.multiple_of(step * SUB, SUB)
            reached = rowmask[2, pl.ds(first, SUB), :]
            for j in range(SUB):
                t = first + j
                state = [lam3[n] * state[n] for n in range(modes)]
                terms = list(state)
                while len(terms) > 1:
                    terms = [a + b for a, b in zip(terms[::2], terms[1::2])]
                f3[t] = f3[t] + terms[0] * reached[j : j + 1, :]
            return state

        lax.fori_loop(0, rows // SUB, body, state)

    for g in range(SUB):
        cols = slice(g * LANE, (g + 1) * LANE)
        out[:, cols] = (outer[:, cols] * scale[...] * f3[:, g, :]).astype(out.dtype)


def params(mib):
    return pltpu.CompilerParams(vmem_limit_bytes=mib << 20)


def fitted(stream, in_weight, pole_rate, residue, skip_gain, doc_lengths, reach):
    rows, depth = stream.shape
    width, _, local = in_weight.shape
    modes = pole_rate.shape[1]
    size = lax.axis_size("ch")
    wt = jnp.transpose(in_weight, (1, 0, 2))
    rate, res = pole_rate.T, residue.T
    f32, b16 = jnp.float32, jnp.bfloat16
    dma = pltpu.SemaphoreType.DMA

    def swap(block, mask):
        return lax.ppermute(block, "ch", [(i, i ^ mask) for i in range(size)])

    def split(block, first):
        masks = (2, 4) if first else (4, 2)
        return lax.ppermute(block, "ch", [(i, i ^ masks[i & 1]) for i in range(size)])

    def call(kernel, ins, outs, scratch, flops, mib):
        return pl.pallas_call(
            kernel,
            in_specs=[spec for spec, _ in ins],
            out_specs=[IN_VMEM] * len(outs),
            out_shape=outs,
            scratch_shapes=scratch,
            compiler_params=params(mib),
            cost_estimate=pl.CostEstimate(
                flops=2 * rows * depth * local * flops, bytes_accessed=0, transcendentals=0
            ),
            name=kernel.__name__,
        )(*[array for _, array in ins])

    def here(*arrays):
        return [(IN_VMEM, a) for a in arrays]

    planes = pltpu.VMEM((2, rows, local), f32)
    product = pltpu.VMEM((rows, local), f32)
    squares = pltpu.VMEM((rows, LANE), f32)
    poles = pltpu.VMEM((modes, SUB, LANE), f32)
    tokens = pltpu.VMEM((rows, SUB, LANE), f32)
    chunk = pltpu.VMEM((rows, depth), b16)
    vector = pltpu.VMEM((modes, local), f32)

    def there(*arrays):
        return [(IN_HBM, pltpu.with_memory_space_constraint(a, pltpu.HBM)) for a in arrays]

    def weights(planes_of, chunks):
        return pltpu.VMEM((planes_of, chunks * depth, local), b16)

    s = swap(stream, 1)
    a, b, d = split(stream, True), split(stream, False), swap(stream, 6)
    acc, outer, sq, lam3, mix3, near, far, gate_a, rowmask, valid = call(
        first_kernel,
        there(stream) + here(s) + there(wt, rate, res, doc_lengths),
        [planes, product, squares, poles, poles, weights(2, 3), weights(2, 2), weights(1, 1)]
        + [pltpu.VMEM((3, rows, LANE), f32), pltpu.VMEM((reach, SUB, LANE), f32)],
        [chunk, weights(2, 2), weights(1, 2), vector, vector, pltpu.SMEM(doc_lengths.shape, jnp.int32), dma((17,)), dma((4,))],
        4,
        16,
    )
    a, b, d, acc, sq = lax.optimization_barrier((a, b, d, acc, sq))
    ao, bo, do = swap(a, 1), swap(b, 1), swap(d, 1)
    acc, sq, far_d = call(
        near_kernel,
        here(a, b, d, near) + there(wt) + here(acc, sq),
        [planes, squares, weights(2, 1)],
        [dma((2,))],
        6,
        4,
    )
    scale, d3, e3, gate_far = call(
        far_kernel,
        here(ao, bo, do, far, far_d) + there(wt) + here(acc, sq, lam3, rowmask),
        [squares, tokens, poles, weights(1, 3)],
        [planes, dma((3,))],
        6,
        4,
    )
    ring = lax.axis_size("ctx")
    arrived = [
        lax.ppermute(e3, "ctx", [(i, (i + k) % ring) for i in range(ring)])
        for k in range(1, reach + 1)
    ]
    outer, f3 = call(
        outer_kernel,
        here(a, b, d, ao, bo, do)
        + there(wt)
        + here(outer, gate_a, gate_far, d3, lam3, mix3, skip_gain.reshape(SUB, LANE), rowmask),
        [product, tokens],
        [weights(1, 2), dma((2,))],
        8,
        16,
    )
    return pl.pallas_call(
        functools.partial(last_kernel, count=reach),
        in_specs=[IN_VMEM] * (reach + 7),
        out_specs=IN_VMEM,
        out_shape=jax.ShapeDtypeStruct((rows, local), b16),
        compiler_params=params(8),
        name="last",
    )(*arrived, outer, f3, scale, lam3, mix3, rowmask, valid)


def solution(mesh):
    placed = (P("ctx", "ch"), P(None, None, "ch"), P("ch", None), P("ch", None), P("ch"), P())
    ring = mesh.shape["ctx"]

    def per_device(*args):
        stream, in_weight = args[0], args[1]
        rows, depth = stream.shape
        longest = rows * ring // 2
        reach = min(ring - 1, (longest + rows - 2) // rows)
        if mesh.shape["ch"] == 8 and in_weight.shape[2] == SUB * LANE and rows == LANE:
            return fitted(*args, reach)
        return general(*args)

    return jax.shard_map(
        per_device, mesh=mesh, in_specs=placed, out_specs=P("ctx", "ch"), check_vma=False
    )
```

```python
import functools

import jax
import jax.numpy as jnp
from jax import lax
from jax.experimental import pallas as pl
from jax.experimental.pallas import tpu as pltpu
from jax.sharding import PartitionSpec as P

SUB = 8
LANE = 128
IN_VMEM = pl.BlockSpec(memory_space=pltpu.VMEM)
IN_HBM = pl.BlockSpec(memory_space=pltpu.HBM)
DRIVEN = (1, 2)
GATE = (0,)


def shifted(block, axis, distance):
    devices = range(lax.axis_size(axis))
    route = [(i - distance, i) for i in devices if i - distance in devices]
    return lax.ppermute(block, axis, route)


def combine(earlier, later):
    return (earlier[0] * later[0], later[0] * earlier[1] + later[1])


def split_proj(product, squares, width, local):
    rowscale = lax.rsqrt(squares / width + 1e-06)
    proj = product * rowscale[:, None]
    outer = proj[:, :local]
    driven = proj[:, local : 2 * local] * proj[:, 2 * local :]
    return (outer, driven)


def local_scan(driven, keep, lam):
    modes, local = lam.shape
    decay = keep[:, None, None] * lam[None, :, :]
    drive = jnp.broadcast_to(driven[:, None, :], (driven.shape[0], modes, local))
    return lax.associative_scan(combine, (decay, drive), axis=0)


def general(stream, in_weight, pole_rate, residue, skip_gain, doc_lengths):
    rows = stream.shape[0]
    width = in_weight.shape[0]
    local = in_weight.shape[2]
    modes = pole_rate.shape[1]
    weights = in_weight.reshape(width, 3 * local)
    lam = jnp.exp(-pole_rate).T
    mix = (residue * jnp.sqrt(-jnp.expm1(-2.0 * pole_rate))).T
    starts = jnp.cumsum(doc_lengths) - doc_lengths
    position = lax.axis_index("ctx") * rows + jnp.arange(rows, dtype=jnp.int32)
    is_start = jnp.any(position[:, None] == starts[None, :], axis=1)
    keep = jnp.where(is_start, 0.0, 1.0).astype(jnp.float32)
    whole = lax.all_gather(stream, "ch", axis=1, tiled=True)
    floats = whole.astype(jnp.float32)
    squares = jnp.sum(floats * floats, axis=1)
    product = jnp.dot(whole, weights, preferred_element_type=jnp.float32)
    outer, driven = split_proj(product, squares, width, local)
    decay_cum, local_state = local_scan(driven, keep, lam)
    block_decay = decay_cum[-1]
    block_state = local_state[-1]
    zeros_state = jnp.zeros((modes, local), jnp.float32)

    def forward(step, incoming):
        outgoing = block_decay * incoming + block_state
        return shifted(outgoing, "ctx", 1)

    incoming = lax.fori_loop(0, lax.axis_size("ctx") - 1, forward, zeros_state)
    state = local_state + decay_cum * incoming[None, :, :]
    filtered = jnp.einsum("tnc,nc->tc", state, mix)
    return (outer * (filtered + skip_gain[None, :] * driven)).astype(jnp.bfloat16)


def chunk_rows(mask, depth):
    return pl.ds(pl.multiple_of((lax.axis_index("ch") ^ mask) * depth, depth), depth)


def add_squares(sq, blocks):
    total = sq
    for ref in blocks:
        for g in range(ref.shape[1] // LANE):
            v = ref[:, g * LANE : (g + 1) * LANE].astype(jnp.float32)
            total = total + v * v
    return total


def by_groups(value, store):
    for g in range(SUB):
        store(g, value[:, g * LANE : (g + 1) * LANE])


def dot(a, b):
    return jnp.dot(a, b, preferred_element_type=jnp.float32)


def run_copies(copies, ahead):
    for c in copies[:ahead]:
        c.start()

    def wait(i):
        copies[i].wait()
        if i + ahead < len(copies):
            copies[i + ahead].start()

    return wait


def weight_copies(wt, planes, masks, depth, target, sem, at=0):
    return [
        pltpu.make_async_copy(
            wt.at[p, chunk_rows(m, depth)],
            target.at[k, pl.ds(i * depth, depth)],
            sem.at[at + k * len(masks) + i],
        )
        for k, p in enumerate(planes)
        for i, m in enumerate(masks)
    ]


def project(blocks, weights, plane):
    depth = blocks[0].shape[1]
    total = dot(blocks[0][...], weights[plane, :depth])
    for i in range(1, len(blocks)):
        total = total + dot(blocks[i][...], weights[plane, i * depth : (i + 1) * depth])
    return total


def own_masks():
    core = lax.axis_index("ch") & 1
    one, two = 2 + 2 * core, 4 - 2 * core
    return (one, two, 6)


def other_masks():
    core = lax.axis_index("ch") & 1
    one, two = 2 + 2 * core, 4 - 2 * core
    return (two ^ 1, one ^ 1, 7)


def first_kernel(
    o, s, wt, rate, res, lengths, acc, outer, sq, lam3, mix3, near, far, gate, rowmask, valid, held, wbuf, gbuf, rates, ress, docs, sem, small
):
    rows, depth = s.shape
    own = [
        pltpu.make_async_copy(o, held, small.at[0]),
        pltpu.make_async_copy(rate, rates, small.at[1]),
        pltpu.make_async_copy(res, ress, small.at[2]),
        pltpu.make_async_copy(lengths, docs, small.at[3]),
    ]
    copies = weight_copies(wt, DRIVEN, (0, 1), depth, wbuf, sem)
    copies += weight_copies(wt, GATE, (0, 1), depth, gbuf, sem, 4)
    copies += weight_copies(wt, DRIVEN, own_masks(), depth, near, sem, 6)
    copies += weight_copies(wt, DRIVEN, other_masks()[:2], depth, far, sem, 12)
    copies += weight_copies(wt, GATE, own_masks()[:1], depth, gate, sem, 16)
    run_copies(own, len(own))
    wait = run_copies(copies, 8)
    for c in own:
        c.wait()
    blocks = (held, s)
    sq[...] = add_squares(jnp.zeros(sq.shape, jnp.float32), blocks)
    r = rates[...]
    lam = jnp.exp(-r)
    tanh = jnp.tanh(r)
    mix = ress[...] * jnp.sqrt(2.0 * tanh / (1.0 + tanh))

    def put_lam(g, v):
        lam3[:, g, :] = v

    def put_mix(g, v):
        mix3[:, g, :] = v

    by_groups(lam, put_lam)
    by_groups(mix, put_mix)
    mark_rows(docs, rows, rowmask, valid)
    for k in range(2):
        wait(2 * k)
        wait(2 * k + 1)
        acc[k] = project(blocks, wbuf, k)
    wait(4)
    wait(5)
    outer[...] = project(blocks, gbuf, 0)
    for i in range(6, len(copies)):
        wait(i)


def near_kernel(a, b, d, weights, wt, acc_in, sq_in, acc, sq, far, sem):
    blocks = (a, b, d)
    wait = run_copies(weight_copies(wt, DRIVEN, other_masks()[2:], a.shape[1], far, sem), 8)
    sq[...] = add_squares(sq_in[...], blocks)

    @pl.loop(0, 2)
    def _(k):
        acc[k] = acc_in[k] + project(blocks, weights, k)

    for i in range(2):
        wait(i)


def far_kernel(
    a, b, d, weights, last_weights, wt, acc_in, sq_in, lam3, rowmask, scale, d3, e3, gate, both, sem
):
    rows, depth = a.shape
    wait = run_copies(weight_copies(wt, GATE, own_masks()[1:] + other_masks()[:1], depth, gate, sem), 8)
    blocks = (a, b, d)
    total = jnp.sum(add_squares(sq_in[...], blocks), axis=1, keepdims=True)
    row = lax.rsqrt(total / (8 * depth) + 1e-06)
    scale[...] = jnp.broadcast_to(row, scale.shape)

    @pl.loop(0, 2)
    def _(k):
        both[k] = acc_in[k] + project((a, b), weights, k) + project((d,), last_weights, k)

    for g in range(SUB):
        cols = slice(g * LANE, (g + 1) * LANE)
        d3[:, g, :] = (both[0, :, cols] * scale[...]) * (both[1, :, cols] * scale[...])
    modes = lam3.shape[0]

    def body(step, state):
        first = pl.multiple_of(step * SUB, SUB)
        counts = rowmask[0, pl.ds(first, SUB), :]
        for j in range(SUB):
            drive = d3[first + j] * counts[j : j + 1, :]
            state = [lam3[n] * state[n] + drive for n in range(modes)]
        return state

    zeros = [jnp.zeros((SUB, LANE), jnp.float32) for _ in range(modes)]
    state = lax.fori_loop(0, rows // SUB, body, zeros)
    for n in range(modes):
        e3[n] = state[n]
    for i in range(3):
        wait(i)


def mark_rows(docs, rows, rowmask, valid):
    me = lax.axis_index("ctx")
    at = -me * rows
    first, last, starts = rows, -1, []
    for i in range(docs.shape[0]):
        inside = jnp.logical_and(at >= 0, at < rows)
        first = jnp.where(jnp.logical_and(inside, at < first), at, first)
        last = jnp.where(jnp.logical_and(inside, at > last), at, last)
        starts.append(at)
        at = at + docs[i]
    token = lax.broadcasted_iota(jnp.int32, rowmask.shape[1:], 0)
    rowmask[0] = jnp.where(token >= last, 1.0, 0.0)
    keep = jnp.ones(rowmask.shape[1:], jnp.float32)
    for at in starts:
        keep = jnp.where(token == at, 0.0, keep)
    rowmask[1] = keep
    rowmask[2] = jnp.where(token < first, 1.0, 0.0)
    reached = me >= 1
    for k in range(valid.shape[0]):
        if k > 0:
            for at in starts:
                between = jnp.logical_and(at >= -k * rows, at < -(k - 1) * rows)
                reached = jnp.logical_and(reached, jnp.logical_not(between))
            reached = jnp.logical_and(reached, me >= k + 1)
        valid[k] = jnp.full(valid.shape[1:], jnp.where(reached, 1.0, 0.0))


def outer_kernel(
    a, b, d, ao, bo, do, wt, sum_in, gate_a, gate_far, d3, lam3, mix3, skip, rowmask, outer, f3, wbuf, sem
):
    rows, depth = a.shape
    modes = lam3.shape[0]
    wait = run_copies(weight_copies(wt, GATE, other_masks()[1:], depth, wbuf, sem), 8)

    def body(step, state):
        first = pl.multiple_of(step * SUB, SUB)
        keeps = rowmask[1, pl.ds(first, SUB), :]
        for j in range(SUB):
            drive = d3[first + j]
            state = [lam3[n] * (state[n] * keeps[j : j + 1, :]) + drive for n in range(modes)]
            terms = [mix3[n] * state[n] for n in range(modes)]
            while len(terms) > 1:
                terms = [p + q for p, q in zip(terms[::2], terms[1::2])]
            f3[first + j] = terms[0] + skip[...] * drive
        return state

    zeros = [jnp.zeros((SUB, LANE), jnp.float32) for _ in range(modes)]
    lax.fori_loop(0, rows // SUB, body, zeros)
    total = sum_in[...] + project((a,), gate_a, 0) + project((b, d, ao), gate_far, 0)
    wait(0)
    wait(1)
    outer[...] = total + project((bo, do), wbuf, 0)


def last_kernel(*refs, count):
    arrived = refs[:count]
    outer, f3, scale, lam3, mix3, rowmask, valid, out = refs[count:]
    rows = outer.shape[0]
    modes = lam3.shape[0]
    @pl.when(lax.axis_index("ctx") > 0)
    def _():
        state = []
        for n in range(modes):
            lam = lam3[n]
            whole = lam
            for _ in range(rows.bit_length() - 1):
                whole = whole * whole
            power, total = valid[0], jnp.zeros((SUB, LANE), jnp.float32)
            for k in range(count):
                total = total + power * arrived[k][n].astype(jnp.float32)
                if k + 1 < count:
                    power = valid[k + 1] * whole if k == 0 else valid[k + 1] * (power * whole)
            state.append(mix3[n] * total)

        def body(step, state):
            first = pl.multiple_of(step * SUB, SUB)
            reached = rowmask[2, pl.ds(first, SUB), :]
            for j in range(SUB):
                t = first + j
                state = [lam3[n] * state[n] for n in range(modes)]
                terms = list(state)
                while len(terms) > 1:
                    terms = [a + b for a, b in zip(terms[::2], terms[1::2])]
                f3[t] = f3[t] + terms[0] * reached[j : j + 1, :]
            return state

        lax.fori_loop(0, rows // SUB, body, state)

    for g in range(SUB):
        cols = slice(g * LANE, (g + 1) * LANE)
        out[:, cols] = (outer[:, cols] * scale[...] * f3[:, g, :]).astype(out.dtype)


def params(mib):
    return pltpu.CompilerParams(vmem_limit_bytes=mib << 20)


def fitted(stream, in_weight, pole_rate, residue, skip_gain, doc_lengths, reach):
    rows, depth = stream.shape
    width, _, local = in_weight.shape
    modes = pole_rate.shape[1]
    size = lax.axis_size("ch")
    wt = jnp.transpose(in_weight, (1, 0, 2))
    rate, res = pole_rate.T, residue.T
    f32, b16 = jnp.float32, jnp.bfloat16
    dma = pltpu.SemaphoreType.DMA

    def swap(block, mask):
        return lax.ppermute(block, "ch", [(i, i ^ mask) for i in range(size)])

    def split(block, first):
        masks = (2, 4) if first else (4, 2)
        return lax.ppermute(block, "ch", [(i, i ^ masks[i & 1]) for i in range(size)])

    def call(kernel, ins, outs, scratch, flops, mib):
        return pl.pallas_call(
            kernel,
            in_specs=[spec for spec, _ in ins],
            out_specs=[IN_VMEM] * len(outs),
            out_shape=outs,
            scratch_shapes=scratch,
            compiler_params=params(mib),
            cost_estimate=pl.CostEstimate(
                flops=2 * rows * depth * local * flops, bytes_accessed=0, transcendentals=0
            ),
            name=kernel.__name__,
        )(*[array for _, array in ins])

    def here(*arrays):
        return [(IN_VMEM, a) for a in arrays]

    planes = pltpu.VMEM((2, rows, local), f32)
    product = pltpu.VMEM((rows, local), f32)
    squares = pltpu.VMEM((rows, LANE), f32)
    poles = pltpu.VMEM((modes, SUB, LANE), f32)
    tokens = pltpu.VMEM((rows, SUB, LANE), f32)
    chunk = pltpu.VMEM((rows, depth), b16)
    vector = pltpu.VMEM((modes, local), f32)

    def there(*arrays):
        return [(IN_HBM, pltpu.with_memory_space_constraint(a, pltpu.HBM)) for a in arrays]

    def weights(planes_of, chunks):
        return pltpu.VMEM((planes_of, chunks * depth, local), b16)

    s = swap(stream, 1)
    a, b, d = split(stream, True), split(stream, False), swap(stream, 6)
    acc, outer, sq, lam3, mix3, near, far, gate_a, rowmask, valid = call(
        first_kernel,
        there(stream) + here(s) + there(wt, rate, res, doc_lengths),
        [planes, product, squares, poles, poles, weights(2, 3), weights(2, 2), weights(1, 1)]
        + [pltpu.VMEM((3, rows, LANE), f32), pltpu.VMEM((reach, SUB, LANE), f32)],
        [chunk, weights(2, 2), weights(1, 2), vector, vector, pltpu.SMEM(doc_lengths.shape, jnp.int32), dma((17,)), dma((4,))],
        4,
        16,
    )
    a, b, d, acc, sq = lax.optimization_barrier((a, b, d, acc, sq))
    ao, bo, do = swap(a, 1), swap(b, 1), swap(d, 1)
    acc, sq, far_d = call(
        near_kernel,
        here(a, b, d, near) + there(wt) + here(acc, sq),
        [planes, squares, weights(2, 1)],
        [dma((2,))],
        6,
        4,
    )
    scale, d3, e3, gate_far = call(
        far_kernel,
        here(ao, bo, do, far, far_d) + there(wt) + here(acc, sq, lam3, rowmask),
        [squares, tokens, poles, weights(1, 3)],
        [planes, dma((3,))],
        6,
        4,
    )
    ring = lax.axis_size("ctx")
    arrived = [
        lax.ppermute(e3 if k == 1 else e3.astype(b16), "ctx", [(i, (i + k) % ring) for i in range(ring)])
        for k in range(1, reach + 1)
    ]
    outer, f3 = call(
        outer_kernel,
        here(a, b, d, ao, bo, do)
        + there(wt)
        + here(outer, gate_a, gate_far, d3, lam3, mix3, skip_gain.reshape(SUB, LANE), rowmask),
        [product, tokens],
        [weights(1, 2), dma((2,))],
        8,
        16,
    )
    return pl.pallas_call(
        functools.partial(last_kernel, count=reach),
        in_specs=[IN_VMEM] * (reach + 7),
        out_specs=IN_VMEM,
        out_shape=jax.ShapeDtypeStruct((rows, local), b16),
        compiler_params=params(8),
        name="last",
    )(*arrived, outer, f3, scale, lam3, mix3, rowmask, valid)


def solution(mesh):
    placed = (P("ctx", "ch"), P(None, None, "ch"), P("ch", None), P("ch", None), P("ch"), P())
    ring = mesh.shape["ctx"]

    def per_device(*args):
        stream, in_weight = args[0], args[1]
        rows, depth = stream.shape
        longest = rows * ring // 2
        reach = min(ring - 1, (longest + rows - 2) // rows)
        if mesh.shape["ch"] == 8 and in_weight.shape[2] == SUB * LANE and rows == LANE:
            return fitted(*args, reach)
        return general(*args)

    return jax.shard_map(
        per_device, mesh=mesh, in_specs=placed, out_specs=P("ctx", "ch"), check_vma=False
    )
```

```python
import functools

import jax
import jax.numpy as jnp
from jax import lax
from jax.experimental import pallas as pl
from jax.experimental.pallas import tpu as pltpu
from jax.sharding import PartitionSpec as P

SUB = 8
LANE = 128
IN_VMEM = pl.BlockSpec(memory_space=pltpu.VMEM)
IN_HBM = pl.BlockSpec(memory_space=pltpu.HBM)
DRIVEN = (1, 2)
GATE = (0,)


def shifted(block, axis, distance):
    devices = range(lax.axis_size(axis))
    route = [(i - distance, i) for i in devices if i - distance in devices]
    return lax.ppermute(block, axis, route)


def combine(earlier, later):
    return (earlier[0] * later[0], later[0] * earlier[1] + later[1])


def split_proj(product, squares, width, local):
    rowscale = lax.rsqrt(squares / width + 1e-06)
    proj = product * rowscale[:, None]
    outer = proj[:, :local]
    driven = proj[:, local : 2 * local] * proj[:, 2 * local :]
    return (outer, driven)


def local_scan(driven, keep, lam):
    modes, local = lam.shape
    decay = keep[:, None, None] * lam[None, :, :]
    drive = jnp.broadcast_to(driven[:, None, :], (driven.shape[0], modes, local))
    return lax.associative_scan(combine, (decay, drive), axis=0)


def general(stream, in_weight, pole_rate, residue, skip_gain, doc_lengths):
    rows = stream.shape[0]
    width = in_weight.shape[0]
    local = in_weight.shape[2]
    modes = pole_rate.shape[1]
    weights = in_weight.reshape(width, 3 * local)
    lam = jnp.exp(-pole_rate).T
    mix = (residue * jnp.sqrt(-jnp.expm1(-2.0 * pole_rate))).T
    starts = jnp.cumsum(doc_lengths) - doc_lengths
    position = lax.axis_index("ctx") * rows + jnp.arange(rows, dtype=jnp.int32)
    is_start = jnp.any(position[:, None] == starts[None, :], axis=1)
    keep = jnp.where(is_start, 0.0, 1.0).astype(jnp.float32)
    whole = lax.all_gather(stream, "ch", axis=1, tiled=True)
    floats = whole.astype(jnp.float32)
    squares = jnp.sum(floats * floats, axis=1)
    product = jnp.dot(whole, weights, preferred_element_type=jnp.float32)
    outer, driven = split_proj(product, squares, width, local)
    decay_cum, local_state = local_scan(driven, keep, lam)
    block_decay = decay_cum[-1]
    block_state = local_state[-1]
    zeros_state = jnp.zeros((modes, local), jnp.float32)

    def forward(step, incoming):
        outgoing = block_decay * incoming + block_state
        return shifted(outgoing, "ctx", 1)

    incoming = lax.fori_loop(0, lax.axis_size("ctx") - 1, forward, zeros_state)
    state = local_state + decay_cum * incoming[None, :, :]
    filtered = jnp.einsum("tnc,nc->tc", state, mix)
    return (outer * (filtered + skip_gain[None, :] * driven)).astype(jnp.bfloat16)


def chunk_rows(mask, depth):
    return pl.ds(pl.multiple_of((lax.axis_index("ch") ^ mask) * depth, depth), depth)


def add_squares(sq, blocks):
    total = sq
    for ref in blocks:
        for g in range(ref.shape[1] // LANE):
            v = ref[:, g * LANE : (g + 1) * LANE].astype(jnp.float32)
            total = total + v * v
    return total


def by_groups(value, store):
    for g in range(SUB):
        store(g, value[:, g * LANE : (g + 1) * LANE])


def dot(a, b):
    return jnp.dot(a, b, preferred_element_type=jnp.float32)


def run_copies(copies, ahead):
    for c in copies[:ahead]:
        c.start()

    def wait(i):
        copies[i].wait()
        if i + ahead < len(copies):
            copies[i + ahead].start()

    return wait


def weight_copies(wt, planes, masks, depth, target, sem, at=0):
    return [
        pltpu.make_async_copy(
            wt.at[p, chunk_rows(m, depth)],
            target.at[k, pl.ds(i * depth, depth)],
            sem.at[at + k * len(masks) + i],
        )
        for k, p in enumerate(planes)
        for i, m in enumerate(masks)
    ]


def project(blocks, weights, plane):
    depth = blocks[0].shape[1]
    total = dot(blocks[0][...], weights[plane, :depth])
    for i in range(1, len(blocks)):
        total = total + dot(blocks[i][...], weights[plane, i * depth : (i + 1) * depth])
    return total


def own_masks():
    core = lax.axis_index("ch") & 1
    one, two = 4 - 2 * core, 2 + 2 * core
    return (one, two, 6)


def other_masks():
    core = lax.axis_index("ch") & 1
    one, two = 4 - 2 * core, 2 + 2 * core
    return (two ^ 1, one ^ 1, 7)


def first_kernel(
    o, s, wt, rate, res, lengths, acc, outer, sq, lam3, mix3, near, far, rowmask, valid, held, wbuf, gbuf, rates, ress, docs, sem, small
):
    rows, depth = s.shape
    own = [
        pltpu.make_async_copy(o, held, small.at[0]),
        pltpu.make_async_copy(rate, rates, small.at[1]),
        pltpu.make_async_copy(res, ress, small.at[2]),
        pltpu.make_async_copy(lengths, docs, small.at[3]),
    ]
    copies = weight_copies(wt, DRIVEN, (0, 1), depth, wbuf, sem)
    copies += weight_copies(wt, GATE, (0, 1), depth, gbuf, sem, 4)
    copies += weight_copies(wt, DRIVEN, own_masks(), depth, near, sem, 6)
    copies += weight_copies(wt, DRIVEN, other_masks()[:2], depth, far, sem, 12)
    run_copies(own, len(own))
    wait = run_copies(copies, 8)
    for c in own:
        c.wait()
    blocks = (held, s)
    sq[...] = add_squares(jnp.zeros(sq.shape, jnp.float32), blocks)
    r = rates[...]
    lam = jnp.exp(-r)
    tanh = jnp.tanh(r)
    mix = ress[...] * jnp.sqrt(2.0 * tanh / (1.0 + tanh))

    def put_lam(g, v):
        lam3[:, g, :] = v

    def put_mix(g, v):
        mix3[:, g, :] = v

    by_groups(lam, put_lam)
    by_groups(mix, put_mix)
    mark_rows(docs, rows, rowmask, valid)
    for k in range(2):
        wait(2 * k)
        wait(2 * k + 1)
        acc[k] = project(blocks, wbuf, k)
    wait(4)
    wait(5)
    outer[...] = project(blocks, gbuf, 0)
    for i in range(6, len(copies)):
        wait(i)


def near_kernel(a, b, d, weights, wt, acc_in, sq_in, acc, sq, far, sem):
    blocks = (a, b, d)
    wait = run_copies(weight_copies(wt, DRIVEN, other_masks()[2:], a.shape[1], far, sem), 8)
    sq[...] = add_squares(sq_in[...], blocks)

    @pl.loop(0, 2)
    def _(k):
        acc[k] = acc_in[k] + project(blocks, weights, k)

    for i in range(2):
        wait(i)


def far_kernel(
    weights, a, b, d, last_weights, wt, acc_in, sq_in, lam3, rowmask, scale, d3, e3, gate, both, sem
):
    rows, depth = a.shape
    wait = run_copies(weight_copies(wt, GATE, own_masks()[1:] + other_masks()[:1], depth, gate, sem), 8)
    blocks = (a, b, d)
    total = jnp.sum(add_squares(sq_in[...], blocks), axis=1, keepdims=True)
    row = lax.rsqrt(total / (8 * depth) + 1e-06)
    scale[...] = jnp.broadcast_to(row, scale.shape)

    @pl.loop(0, 2)
    def _(k):
        both[k] = acc_in[k] + project((a, b), weights, k) + project((d,), last_weights, k)

    for g in range(SUB):
        cols = slice(g * LANE, (g + 1) * LANE)
        d3[:, g, :] = (both[0, :, cols] * scale[...]) * (both[1, :, cols] * scale[...])
    modes = lam3.shape[0]

    def body(step, state):
        first = pl.multiple_of(step * SUB, SUB)
        counts = rowmask[0, pl.ds(first, SUB), :]
        for j in range(SUB):
            drive = d3[first + j] * counts[j : j + 1, :]
            state = [lam3[n] * state[n] + drive for n in range(modes)]
        return state

    zeros = [jnp.zeros((SUB, LANE), jnp.float32) for _ in range(modes)]
    state = lax.fori_loop(0, rows // SUB, body, zeros)
    for n in range(modes):
        e3[n] = state[n]
    for i in range(3):
        wait(i)


def mark_rows(docs, rows, rowmask, valid):
    me = lax.axis_index("ctx")
    at = -me * rows
    first, last, starts = rows, -1, []
    for i in range(docs.shape[0]):
        inside = jnp.logical_and(at >= 0, at < rows)
        first = jnp.where(jnp.logical_and(inside, at < first), at, first)
        last = jnp.where(jnp.logical_and(inside, at > last), at, last)
        starts.append(at)
        at = at + docs[i]
    token = lax.broadcasted_iota(jnp.int32, rowmask.shape[1:], 0)
    rowmask[0] = jnp.where(token >= last, 1.0, 0.0)
    keep = jnp.ones(rowmask.shape[1:], jnp.float32)
    for at in starts:
        keep = jnp.where(token == at, 0.0, keep)
    rowmask[1] = keep
    rowmask[2] = jnp.where(token < first, 1.0, 0.0)
    reached = me >= 1
    for k in range(valid.shape[0]):
        if k > 0:
            for at in starts:
                between = jnp.logical_and(at >= -k * rows, at < -(k - 1) * rows)
                reached = jnp.logical_and(reached, jnp.logical_not(between))
            reached = jnp.logical_and(reached, me >= k + 1)
        valid[k] = jnp.full(valid.shape[1:], jnp.where(reached, 1.0, 0.0))


def outer_kernel(
    a, b, d, ao, bo, do, wt, sum_in, gate_far, d3, lam3, mix3, skip, rowmask, outer, f3, wbuf, sem
):
    rows, depth = a.shape
    modes = lam3.shape[0]
    wait = run_copies(weight_copies(wt, GATE, own_masks()[:1] + other_masks()[1:], depth, wbuf, sem), 8)

    def body(step, state):
        first = pl.multiple_of(step * SUB, SUB)
        keeps = rowmask[1, pl.ds(first, SUB), :]
        for j in range(SUB):
            drive = d3[first + j]
            state = [lam3[n] * (state[n] * keeps[j : j + 1, :]) + drive for n in range(modes)]
            terms = [mix3[n] * state[n] for n in range(modes)]
            while len(terms) > 1:
                terms = [p + q for p, q in zip(terms[::2], terms[1::2])]
            f3[first + j] = terms[0] + skip[...] * drive
        return state

    zeros = [jnp.zeros((SUB, LANE), jnp.float32) for _ in range(modes)]
    lax.fori_loop(0, rows // SUB, body, zeros)
    total = sum_in[...] + project((b, d, ao), gate_far, 0)
    for i, block in enumerate((a, bo, do)):
        wait(i)
        total = total + dot(block[...], wbuf[0, i * depth : (i + 1) * depth])
    outer[...] = total


def last_kernel(*refs, count):
    arrived = refs[:count]
    outer, f3, scale, lam3, mix3, rowmask, valid, out = refs[count:]
    rows = outer.shape[0]
    modes = lam3.shape[0]
    @pl.when(lax.axis_index("ctx") > 0)
    def _():
        state = []
        for n in range(modes):
            lam = lam3[n]
            whole = lam
            for _ in range(rows.bit_length() - 1):
                whole = whole * whole
            power, total = valid[0], jnp.zeros((SUB, LANE), jnp.float32)
            for k in range(count):
                total = total + power * arrived[k][n].astype(jnp.float32)
                if k + 1 < count:
                    power = valid[k + 1] * whole if k == 0 else valid[k + 1] * (power * whole)
            state.append(mix3[n] * total)

        def body(step, state):
            first = pl.multiple_of(step * SUB, SUB)
            reached = rowmask[2, pl.ds(first, SUB), :]
            for j in range(SUB):
                t = first + j
                state = [lam3[n] * state[n] for n in range(modes)]
                terms = list(state)
                while len(terms) > 1:
                    terms = [a + b for a, b in zip(terms[::2], terms[1::2])]
                f3[t] = f3[t] + terms[0] * reached[j : j + 1, :]
            return state

        lax.fori_loop(0, rows // SUB, body, state)

    for g in range(SUB):
        cols = slice(g * LANE, (g + 1) * LANE)
        out[:, cols] = (outer[:, cols] * scale[...] * f3[:, g, :]).astype(out.dtype)


def params(mib):
    return pltpu.CompilerParams(vmem_limit_bytes=mib << 20)


def fitted(stream, in_weight, pole_rate, residue, skip_gain, doc_lengths, reach):
    rows, depth = stream.shape
    width, _, local = in_weight.shape
    modes = pole_rate.shape[1]
    size = lax.axis_size("ch")
    wt = jnp.transpose(in_weight, (1, 0, 2))
    rate, res = pole_rate.T, residue.T
    f32, b16 = jnp.float32, jnp.bfloat16
    dma = pltpu.SemaphoreType.DMA

    def swap(block, mask):
        return lax.ppermute(block, "ch", [(i, i ^ mask) for i in range(size)])

    def split(block, first):
        masks = (4, 2) if first else (2, 4)
        return lax.ppermute(block, "ch", [(i, i ^ masks[i & 1]) for i in range(size)])

    def call(kernel, ins, outs, scratch, flops, mib):
        return pl.pallas_call(
            kernel,
            in_specs=[spec for spec, _ in ins],
            out_specs=[IN_VMEM] * len(outs),
            out_shape=outs,
            scratch_shapes=scratch,
            compiler_params=params(mib),
            cost_estimate=pl.CostEstimate(
                flops=2 * rows * depth * local * flops, bytes_accessed=0, transcendentals=0
            ),
            name=kernel.__name__,
        )(*[array for _, array in ins])

    def here(*arrays):
        return [(IN_VMEM, a) for a in arrays]

    planes = pltpu.VMEM((2, rows, local), f32)
    product = pltpu.VMEM((rows, local), f32)
    squares = pltpu.VMEM((rows, LANE), f32)
    poles = pltpu.VMEM((modes, SUB, LANE), f32)
    tokens = pltpu.VMEM((rows, SUB, LANE), f32)
    chunk = pltpu.VMEM((rows, depth), b16)
    vector = pltpu.VMEM((modes, local), f32)

    def there(*arrays):
        return [(IN_HBM, pltpu.with_memory_space_constraint(a, pltpu.HBM)) for a in arrays]

    def weights(planes_of, chunks):
        return pltpu.VMEM((planes_of, chunks * depth, local), b16)

    s = swap(stream, 1)
    a, b, d = split(stream, True), split(stream, False), swap(stream, 6)
    acc, outer, sq, lam3, mix3, near, far, rowmask, valid = call(
        first_kernel,
        there(stream) + here(s) + there(wt, rate, res, doc_lengths),
        [planes, product, squares, poles, poles, weights(2, 3), weights(2, 2)]
        + [pltpu.VMEM((3, rows, LANE), f32), pltpu.VMEM((reach, SUB, LANE), f32)],
        [chunk, weights(2, 2), weights(1, 2), vector, vector, pltpu.SMEM(doc_lengths.shape, jnp.int32), dma((16,)), dma((4,))],
        4,
        16,
    )
    a, b, d, acc, sq = lax.optimization_barrier((a, b, d, acc, sq))
    ao, bo, do = swap(a, 1), swap(b, 1), swap(d, 1)
    acc, sq, far_d = call(
        near_kernel,
        here(a, b, d, near) + there(wt) + here(acc, sq),
        [planes, squares, weights(2, 1)],
        [dma((2,))],
        6,
        4,
    )
    scale, d3, e3, gate_far = call(
        far_kernel,
        here(far, ao, bo, do, far_d) + there(wt) + here(acc, sq, lam3, rowmask),
        [squares, tokens, poles, weights(1, 3)],
        [planes, dma((3,))],
        6,
        4,
    )
    ring = lax.axis_size("ctx")
    arrived = [
        lax.ppermute(e3 if k == 1 else e3.astype(b16), "ctx", [(i, (i + k) % ring) for i in range(ring)])
        for k in range(1, reach + 1)
    ]
    outer, f3 = call(
        outer_kernel,
        here(a, b, d, ao, bo, do)
        + there(wt)
        + here(outer, gate_far, d3, lam3, mix3, skip_gain.reshape(SUB, LANE), rowmask),
        [product, tokens],
        [weights(1, 3), dma((3,))],
        6,
        16,
    )
    return pl.pallas_call(
        functools.partial(last_kernel, count=reach),
        in_specs=[IN_VMEM] * (reach + 7),
        out_specs=IN_VMEM,
        out_shape=jax.ShapeDtypeStruct((rows, local), b16),
        compiler_params=params(8),
        name="last",
    )(*arrived, outer, f3, scale, lam3, mix3, rowmask, valid)


def solution(mesh):
    placed = (P("ctx", "ch"), P(None, None, "ch"), P("ch", None), P("ch", None), P("ch"), P())
    ring = mesh.shape["ctx"]

    def per_device(*args):
        stream, in_weight = args[0], args[1]
        rows, depth = stream.shape
        longest = rows * ring // 2
        reach = min(ring - 1, (longest + rows - 2) // rows)
        if mesh.shape["ch"] == 8 and in_weight.shape[2] == SUB * LANE and rows == LANE:
            return fitted(*args, reach)
        return general(*args)

    return jax.shard_map(
        per_device, mesh=mesh, in_specs=placed, out_specs=P("ctx", "ch"), check_vma=False
    )
```

```python
import functools

import jax
import jax.numpy as jnp
from jax import lax
from jax.experimental import pallas as pl
from jax.experimental.pallas import tpu as pltpu
from jax.sharding import PartitionSpec as P

SUB = 8
LANE = 128
IN_VMEM = pl.BlockSpec(memory_space=pltpu.VMEM)
IN_HBM = pl.BlockSpec(memory_space=pltpu.HBM)
DRIVEN = (1, 2)
GATE = (0,)


def shifted(block, axis, distance):
    devices = range(lax.axis_size(axis))
    route = [(i - distance, i) for i in devices if i - distance in devices]
    return lax.ppermute(block, axis, route)


def combine(earlier, later):
    return (earlier[0] * later[0], later[0] * earlier[1] + later[1])


def split_proj(product, squares, width, local):
    rowscale = lax.rsqrt(squares / width + 1e-06)
    proj = product * rowscale[:, None]
    outer = proj[:, :local]
    driven = proj[:, local : 2 * local] * proj[:, 2 * local :]
    return (outer, driven)


def local_scan(driven, keep, lam):
    modes, local = lam.shape
    decay = keep[:, None, None] * lam[None, :, :]
    drive = jnp.broadcast_to(driven[:, None, :], (driven.shape[0], modes, local))
    return lax.associative_scan(combine, (decay, drive), axis=0)


def general(stream, in_weight, pole_rate, residue, skip_gain, doc_lengths):
    rows = stream.shape[0]
    width = in_weight.shape[0]
    local = in_weight.shape[2]
    modes = pole_rate.shape[1]
    weights = in_weight.reshape(width, 3 * local)
    lam = jnp.exp(-pole_rate).T
    mix = (residue * jnp.sqrt(-jnp.expm1(-2.0 * pole_rate))).T
    starts = jnp.cumsum(doc_lengths) - doc_lengths
    position = lax.axis_index("ctx") * rows + jnp.arange(rows, dtype=jnp.int32)
    is_start = jnp.any(position[:, None] == starts[None, :], axis=1)
    keep = jnp.where(is_start, 0.0, 1.0).astype(jnp.float32)
    whole = lax.all_gather(stream, "ch", axis=1, tiled=True)
    floats = whole.astype(jnp.float32)
    squares = jnp.sum(floats * floats, axis=1)
    product = jnp.dot(whole, weights, preferred_element_type=jnp.float32)
    outer, driven = split_proj(product, squares, width, local)
    decay_cum, local_state = local_scan(driven, keep, lam)
    block_decay = decay_cum[-1]
    block_state = local_state[-1]
    zeros_state = jnp.zeros((modes, local), jnp.float32)

    def forward(step, incoming):
        outgoing = block_decay * incoming + block_state
        return shifted(outgoing, "ctx", 1)

    incoming = lax.fori_loop(0, lax.axis_size("ctx") - 1, forward, zeros_state)
    state = local_state + decay_cum * incoming[None, :, :]
    filtered = jnp.einsum("tnc,nc->tc", state, mix)
    return (outer * (filtered + skip_gain[None, :] * driven)).astype(jnp.bfloat16)


def chunk_rows(mask, depth):
    return pl.ds(pl.multiple_of((lax.axis_index("ch") ^ mask) * depth, depth), depth)


def add_squares(sq, blocks):
    total = sq
    for ref in blocks:
        for g in range(ref.shape[1] // LANE):
            v = ref[:, g * LANE : (g + 1) * LANE].astype(jnp.float32)
            total = total + v * v
    return total


def by_groups(value, store):
    for g in range(SUB):
        store(g, value[:, g * LANE : (g + 1) * LANE])


def dot(a, b):
    return jnp.dot(a, b, preferred_element_type=jnp.float32)


def run_copies(copies, ahead):
    for c in copies[:ahead]:
        c.start()

    def wait(i):
        copies[i].wait()
        if i + ahead < len(copies):
            copies[i + ahead].start()

    return wait


def weight_copies(wt, planes, masks, depth, target, sem, at=0):
    return [
        pltpu.make_async_copy(
            wt.at[p, chunk_rows(m, depth)],
            target.at[k, pl.ds(i * depth, depth)],
            sem.at[at + k * len(masks) + i],
        )
        for k, p in enumerate(planes)
        for i, m in enumerate(masks)
    ]


def project(blocks, weights, plane):
    depth = blocks[0].shape[1]
    total = dot(blocks[0][...], weights[plane, :depth])
    for i in range(1, len(blocks)):
        total = total + dot(blocks[i][...], weights[plane, i * depth : (i + 1) * depth])
    return total


def own_masks():
    core = lax.axis_index("ch") & 1
    one, two = 4 - 2 * core, 2 + 2 * core
    return (one, two, 6)


def other_masks():
    core = lax.axis_index("ch") & 1
    one, two = 4 - 2 * core, 2 + 2 * core
    return (two ^ 1, one ^ 1, 7)


def first_kernel(
    o, s, wt, rate, res, lengths, acc, outer, sq, lam3, mix3, near, far, rowmask, valid, held, wbuf, gbuf, rates, ress, docs, sem, small
):
    rows, depth = s.shape
    own = [
        pltpu.make_async_copy(o, held, small.at[0]),
        pltpu.make_async_copy(rate, rates, small.at[1]),
        pltpu.make_async_copy(res, ress, small.at[2]),
        pltpu.make_async_copy(lengths, docs, small.at[3]),
    ]
    copies = weight_copies(wt, DRIVEN, (0, 1), depth, wbuf, sem)
    copies += weight_copies(wt, GATE, (0, 1), depth, gbuf, sem, 4)
    copies += weight_copies(wt, DRIVEN, own_masks(), depth, near, sem, 6)
    copies += weight_copies(wt, DRIVEN, other_masks()[:2], depth, far, sem, 12)
    run_copies(own, len(own))
    wait = run_copies(copies, 6)
    for c in own:
        c.wait()
    blocks = (held, s)
    sq[...] = add_squares(jnp.zeros(sq.shape, jnp.float32), blocks)
    r = rates[...]
    lam = jnp.exp(-r)
    tanh = jnp.tanh(r)
    mix = ress[...] * jnp.sqrt(2.0 * tanh / (1.0 + tanh))

    def put_lam(g, v):
        lam3[:, g, :] = v

    def put_mix(g, v):
        mix3[:, g, :] = v

    by_groups(lam, put_lam)
    by_groups(mix, put_mix)
    mark_rows(docs, rows, rowmask, valid)
    for k in range(2):
        wait(2 * k)
        wait(2 * k + 1)
        acc[k] = project(blocks, wbuf, k)
    wait(4)
    wait(5)
    outer[...] = project(blocks, gbuf, 0)
    for i in range(6, len(copies)):
        wait(i)


def pack_kernel(a, b, d, packed):
    for i, ref in enumerate((a, b, d)):
        packed[i] = ref[...]


def near_kernel(packed, weights, wt, acc_in, sq_in, acc, sq, far, sem):
    blocks = [packed.at[i] for i in range(3)]
    wait = run_copies(weight_copies(wt, DRIVEN, other_masks()[2:], packed.shape[2], far, sem), 8)
    sq[...] = add_squares(sq_in[...], blocks)

    @pl.loop(0, 2)
    def _(k):
        acc[k] = acc_in[k] + project(blocks, weights, k)

    for i in range(2):
        wait(i)


def far_kernel(
    weights, packed, last_weights, wt, acc_in, sq_in, lam3, rowmask, scale, d3, e3, gate, both, sem
):
    _, rows, depth = packed.shape
    wait = run_copies(weight_copies(wt, GATE, own_masks()[1:] + other_masks()[:1], depth, gate, sem), 8)
    blocks = [packed.at[i] for i in range(3)]
    total = jnp.sum(add_squares(sq_in[...], blocks), axis=1, keepdims=True)
    row = lax.rsqrt(total / (8 * depth) + 1e-06)
    scale[...] = jnp.broadcast_to(row, scale.shape)

    @pl.loop(0, 2)
    def _(k):
        both[k] = acc_in[k] + project(blocks[:2], weights, k) + project(blocks[2:], last_weights, k)

    for g in range(SUB):
        cols = slice(g * LANE, (g + 1) * LANE)
        d3[:, g, :] = (both[0, :, cols] * scale[...]) * (both[1, :, cols] * scale[...])
    modes = lam3.shape[0]

    def body(step, state):
        first = pl.multiple_of(step * SUB, SUB)
        counts = rowmask[0, pl.ds(first, SUB), :]
        for j in range(SUB):
            drive = d3[first + j] * counts[j : j + 1, :]
            state = [lam3[n] * state[n] + drive for n in range(modes)]
        return state

    zeros = [jnp.zeros((SUB, LANE), jnp.float32) for _ in range(modes)]
    state = lax.fori_loop(0, rows // SUB, body, zeros)
    for n in range(modes):
        e3[n] = state[n]
    for i in range(3):
        wait(i)


def mark_rows(docs, rows, rowmask, valid):
    me = lax.axis_index("ctx")
    at = -me * rows
    first, last, starts = rows, -1, []
    for i in range(docs.shape[0]):
        inside = jnp.logical_and(at >= 0, at < rows)
        first = jnp.where(jnp.logical_and(inside, at < first), at, first)
        last = jnp.where(jnp.logical_and(inside, at > last), at, last)
        starts.append(at)
        at = at + docs[i]
    token = lax.broadcasted_iota(jnp.int32, rowmask.shape[1:], 0)
    rowmask[0] = jnp.where(token >= last, 1.0, 0.0)
    keep = jnp.ones(rowmask.shape[1:], jnp.float32)
    for at in starts:
        keep = jnp.where(token == at, 0.0, keep)
    rowmask[1] = keep
    rowmask[2] = jnp.where(token < first, 1.0, 0.0)
    reached = me >= 1
    for k in range(valid.shape[0]):
        if k > 0:
            for at in starts:
                between = jnp.logical_and(at >= -k * rows, at < -(k - 1) * rows)
                reached = jnp.logical_and(reached, jnp.logical_not(between))
            reached = jnp.logical_and(reached, me >= k + 1)
        valid[k] = jnp.full(valid.shape[1:], jnp.where(reached, 1.0, 0.0))


def outer_kernel(
    own, others, wt, sum_in, gate_far, d3, lam3, mix3, skip, rowmask, outer, f3, wbuf, sem
):
    _, rows, depth = own.shape
    a, b, d = [own.at[i] for i in range(3)]
    ao, bo, do = [others.at[i] for i in range(3)]
    modes = lam3.shape[0]
    wait = run_copies(weight_copies(wt, GATE, own_masks()[:1] + other_masks()[1:], depth, wbuf, sem), 8)

    def body(step, state):
        first = pl.multiple_of(step * SUB, SUB)
        keeps = rowmask[1, pl.ds(first, SUB), :]
        for j in range(SUB):
            drive = d3[first + j]
            state = [lam3[n] * (state[n] * keeps[j : j + 1, :]) + drive for n in range(modes)]
            terms = [mix3[n] * state[n] for n in range(modes)]
            while len(terms) > 1:
                terms = [p + q for p, q in zip(terms[::2], terms[1::2])]
            f3[first + j] = terms[0] + skip[...] * drive
        return state

    zeros = [jnp.zeros((SUB, LANE), jnp.float32) for _ in range(modes)]
    lax.fori_loop(0, rows // SUB, body, zeros)
    total = sum_in[...] + project((b, d, ao), gate_far, 0)
    for i, block in enumerate((a, bo, do)):
        wait(i)
        total = total + dot(block[...], wbuf[0, i * depth : (i + 1) * depth])
    outer[...] = total


def last_kernel(*refs, count):
    arrived = refs[:count]
    outer, f3, scale, lam3, mix3, rowmask, valid, out = refs[count:]
    rows = outer.shape[0]
    modes = lam3.shape[0]
    @pl.when(lax.axis_index("ctx") > 0)
    def _():
        state = []
        for n in range(modes):
            lam = lam3[n]
            whole = lam
            for _ in range(rows.bit_length() - 1):
                whole = whole * whole
            power, total = valid[0], jnp.zeros((SUB, LANE), jnp.float32)
            for k in range(count):
                total = total + power * arrived[k][n].astype(jnp.float32)
                if k + 1 < count:
                    power = valid[k + 1] * whole if k == 0 else valid[k + 1] * (power * whole)
            state.append(mix3[n] * total)

        def body(step, state):
            first = pl.multiple_of(step * SUB, SUB)
            reached = rowmask[2, pl.ds(first, SUB), :]
            for j in range(SUB):
                t = first + j
                state = [lam3[n] * state[n] for n in range(modes)]
                terms = list(state)
                while len(terms) > 1:
                    terms = [a + b for a, b in zip(terms[::2], terms[1::2])]
                f3[t] = f3[t] + terms[0] * reached[j : j + 1, :]
            return state

        lax.fori_loop(0, rows // SUB, body, state)

    for g in range(SUB):
        cols = slice(g * LANE, (g + 1) * LANE)
        out[:, cols] = (outer[:, cols] * scale[...] * f3[:, g, :]).astype(out.dtype)


def params(mib):
    return pltpu.CompilerParams(vmem_limit_bytes=mib << 20)


def fitted(stream, in_weight, pole_rate, residue, skip_gain, doc_lengths, reach):
    rows, depth = stream.shape
    width, _, local = in_weight.shape
    modes = pole_rate.shape[1]
    size = lax.axis_size("ch")
    wt = jnp.transpose(in_weight, (1, 0, 2))
    rate, res = pole_rate.T, residue.T
    f32, b16 = jnp.float32, jnp.bfloat16
    dma = pltpu.SemaphoreType.DMA

    def swap(block, mask):
        return lax.ppermute(block, "ch", [(i, i ^ mask) for i in range(size)])

    def split(block, first):
        masks = (4, 2) if first else (2, 4)
        return lax.ppermute(block, "ch", [(i, i ^ masks[i & 1]) for i in range(size)])

    def call(kernel, ins, outs, scratch, flops, mib):
        return pl.pallas_call(
            kernel,
            in_specs=[spec for spec, _ in ins],
            out_specs=[IN_VMEM] * len(outs),
            out_shape=outs,
            scratch_shapes=scratch,
            compiler_params=params(mib),
            cost_estimate=pl.CostEstimate(
                flops=2 * rows * depth * local * flops, bytes_accessed=0, transcendentals=0
            ),
            name=kernel.__name__,
        )(*[array for _, array in ins])

    def here(*arrays):
        return [(IN_VMEM, a) for a in arrays]

    planes = pltpu.VMEM((2, rows, local), f32)
    product = pltpu.VMEM((rows, local), f32)
    squares = pltpu.VMEM((rows, LANE), f32)
    poles = pltpu.VMEM((modes, SUB, LANE), f32)
    tokens = pltpu.VMEM((rows, SUB, LANE), f32)
    chunk = pltpu.VMEM((rows, depth), b16)
    vector = pltpu.VMEM((modes, local), f32)

    def there(*arrays):
        return [(IN_HBM, pltpu.with_memory_space_constraint(a, pltpu.HBM)) for a in arrays]

    def weights(planes_of, chunks):
        return pltpu.VMEM((planes_of, chunks * depth, local), b16)

    s = swap(stream, 1)
    a, b, d = split(stream, True), split(stream, False), swap(stream, 6)
    acc, outer, sq, lam3, mix3, near, far, rowmask, valid = call(
        first_kernel,
        there(stream) + here(s) + there(wt, rate, res, doc_lengths),
        [planes, product, squares, poles, poles, weights(2, 3), weights(2, 2)]
        + [pltpu.VMEM((3, rows, LANE), f32), pltpu.VMEM((reach, SUB, LANE), f32)],
        [chunk, weights(2, 2), weights(1, 2), vector, vector, pltpu.SMEM(doc_lengths.shape, jnp.int32), dma((16,)), dma((4,))],
        4,
        16,
    )
    a, b, d, acc, sq = lax.optimization_barrier((a, b, d, acc, sq))
    (own,) = call(pack_kernel, here(a, b, d), [pltpu.VMEM((3, rows, depth), b16)], [], 1, 1)
    others = swap(own, 1)
    acc, sq, far_d = call(
        near_kernel,
        here(own, near) + there(wt) + here(acc, sq),
        [planes, squares, weights(2, 1)],
        [dma((2,))],
        6,
        4,
    )
    scale, d3, e3, gate_far = call(
        far_kernel,
        here(far, others, far_d) + there(wt) + here(acc, sq, lam3, rowmask),
        [squares, tokens, poles, weights(1, 3)],
        [planes, dma((3,))],
        6,
        4,
    )
    ring = lax.axis_size("ctx")
    arrived = [
        lax.ppermute(e3 if k == 1 else e3.astype(b16), "ctx", [(i, (i + k) % ring) for i in range(ring)])
        for k in range(1, reach + 1)
    ]
    outer, f3 = call(
        outer_kernel,
        here(own, others)
        + there(wt)
        + here(outer, gate_far, d3, lam3, mix3, skip_gain.reshape(SUB, LANE), rowmask),
        [product, tokens],
        [weights(1, 3), dma((3,))],
        6,
        16,
    )
    return pl.pallas_call(
        functools.partial(last_kernel, count=reach),
        in_specs=[IN_VMEM] * (reach + 7),
        out_specs=IN_VMEM,
        out_shape=jax.ShapeDtypeStruct((rows, local), b16),
        compiler_params=params(8),
        name="last",
    )(*arrived, outer, f3, scale, lam3, mix3, rowmask, valid)


def solution(mesh):
    placed = (P("ctx", "ch"), P(None, None, "ch"), P("ch", None), P("ch", None), P("ch"), P())
    ring = mesh.shape["ctx"]

    def per_device(*args):
        stream, in_weight = args[0], args[1]
        rows, depth = stream.shape
        longest = rows * ring // 2
        reach = min(ring - 1, (longest + rows - 2) // rows)
        if mesh.shape["ch"] == 8 and in_weight.shape[2] == SUB * LANE and rows == LANE:
            return fitted(*args, reach)
        return general(*args)

    return jax.shard_map(
        per_device, mesh=mesh, in_specs=placed, out_specs=P("ctx", "ch"), check_vma=False
    )
```

```python
import functools

import jax
import jax.numpy as jnp
from jax import lax
from jax.experimental import pallas as pl
from jax.experimental.pallas import tpu as pltpu
from jax.sharding import PartitionSpec as P

SUB = 8
LANE = 128
PIECE = 32
IN_VMEM = pl.BlockSpec(memory_space=pltpu.VMEM)
IN_HBM = pl.BlockSpec(memory_space=pltpu.HBM)
DRIVEN = (1, 2)
GATE = (0,)


def shifted(block, axis, distance):
    devices = range(lax.axis_size(axis))
    route = [(i - distance, i) for i in devices if i - distance in devices]
    return lax.ppermute(block, axis, route)


def combine(earlier, later):
    return (earlier[0] * later[0], later[0] * earlier[1] + later[1])


def split_proj(product, squares, width, local):
    rowscale = lax.rsqrt(squares / width + 1e-06)
    proj = product * rowscale[:, None]
    outer = proj[:, :local]
    driven = proj[:, local : 2 * local] * proj[:, 2 * local :]
    return (outer, driven)


def local_scan(driven, keep, lam):
    modes, local = lam.shape
    decay = keep[:, None, None] * lam[None, :, :]
    drive = jnp.broadcast_to(driven[:, None, :], (driven.shape[0], modes, local))
    return lax.associative_scan(combine, (decay, drive), axis=0)


def general(stream, in_weight, pole_rate, residue, skip_gain, doc_lengths):
    rows = stream.shape[0]
    width = in_weight.shape[0]
    local = in_weight.shape[2]
    modes = pole_rate.shape[1]
    weights = in_weight.reshape(width, 3 * local)
    lam = jnp.exp(-pole_rate).T
    mix = (residue * jnp.sqrt(-jnp.expm1(-2.0 * pole_rate))).T
    starts = jnp.cumsum(doc_lengths) - doc_lengths
    position = lax.axis_index("ctx") * rows + jnp.arange(rows, dtype=jnp.int32)
    is_start = jnp.any(position[:, None] == starts[None, :], axis=1)
    keep = jnp.where(is_start, 0.0, 1.0).astype(jnp.float32)
    whole = lax.all_gather(stream, "ch", axis=1, tiled=True)
    floats = whole.astype(jnp.float32)
    squares = jnp.sum(floats * floats, axis=1)
    product = jnp.dot(whole, weights, preferred_element_type=jnp.float32)
    outer, driven = split_proj(product, squares, width, local)
    decay_cum, local_state = local_scan(driven, keep, lam)
    block_decay = decay_cum[-1]
    block_state = local_state[-1]
    zeros_state = jnp.zeros((modes, local), jnp.float32)

    def forward(step, incoming):
        outgoing = block_decay * incoming + block_state
        return shifted(outgoing, "ctx", 1)

    incoming = lax.fori_loop(0, lax.axis_size("ctx") - 1, forward, zeros_state)
    state = local_state + decay_cum * incoming[None, :, :]
    filtered = jnp.einsum("tnc,nc->tc", state, mix)
    return (outer * (filtered + skip_gain[None, :] * driven)).astype(jnp.bfloat16)


def chunk_rows(mask, depth):
    return pl.ds(pl.multiple_of((lax.axis_index("ch") ^ mask) * depth, depth), depth)


def add_squares(sq, blocks):
    total = sq
    for ref in blocks:
        for g in range(ref.shape[1] // LANE):
            v = ref[:, g * LANE : (g + 1) * LANE].astype(jnp.float32)
            total = total + v * v
    return total


def by_groups(value, store):
    for g in range(SUB):
        store(g, value[:, g * LANE : (g + 1) * LANE])


def dot(a, b):
    return jnp.dot(a, b, preferred_element_type=jnp.float32)


def run_copies(copies, ahead):
    for c in copies[:ahead]:
        c.start()

    def wait(i):
        copies[i].wait()
        if i + ahead < len(copies):
            copies[i + ahead].start()

    return wait


def weight_copies(wt, planes, masks, depth, target, sem, at=0):
    return [
        pltpu.make_async_copy(
            wt.at[p, chunk_rows(m, depth)],
            target.at[k, pl.ds(i * depth, depth)],
            sem.at[at + k * len(masks) + i],
        )
        for k, p in enumerate(planes)
        for i, m in enumerate(masks)
    ]


def project(blocks, weights, plane):
    depth = blocks[0].shape[1]
    total = dot(blocks[0][...], weights[plane, :depth])
    for i in range(1, len(blocks)):
        total = total + dot(blocks[i][...], weights[plane, i * depth : (i + 1) * depth])
    return total


def own_masks():
    core = lax.axis_index("ch") & 1
    one, two = 4 - 2 * core, 2 + 2 * core
    return (one, two, 6)


def other_masks():
    core = lax.axis_index("ch") & 1
    one, two = 4 - 2 * core, 2 + 2 * core
    return (two ^ 1, one ^ 1, 7)


def first_kernel(
    o, s, wt, rate, res, lengths, acc, outer, sq, lam3, mix3, near, far, rowmask, valid, held, wbuf, gbuf, rates, ress, docs, sem, small
):
    rows, depth = s.shape
    own = [
        pltpu.make_async_copy(o, held, small.at[0]),
        pltpu.make_async_copy(rate, rates, small.at[1]),
        pltpu.make_async_copy(res, ress, small.at[2]),
        pltpu.make_async_copy(lengths, docs, small.at[3]),
    ]
    copies = weight_copies(wt, DRIVEN, (0, 1), depth, wbuf, sem)
    copies += weight_copies(wt, GATE, (0, 1), depth, gbuf, sem, 4)
    copies += weight_copies(wt, DRIVEN, own_masks(), depth, near, sem, 6)
    copies += weight_copies(wt, DRIVEN, other_masks()[:2], depth, far, sem, 12)
    run_copies(own, len(own))
    wait = run_copies(copies, 6)
    for c in own:
        c.wait()
    blocks = (held, s)
    sq[...] = add_squares(jnp.zeros(sq.shape, jnp.float32), blocks)
    r = rates[...]
    lam = jnp.exp(-r)
    tanh = jnp.tanh(r)
    mix = ress[...] * jnp.sqrt(2.0 * tanh / (1.0 + tanh))

    def put_lam(g, v):
        lam3[:, g, :] = v

    def put_mix(g, v):
        mix3[:, g, :] = v

    by_groups(lam, put_lam)
    by_groups(mix, put_mix)
    mark_rows(docs, rows, rowmask, valid)
    for k in range(2):
        wait(2 * k)
        wait(2 * k + 1)
        acc[k] = project(blocks, wbuf, k)
    wait(4)
    wait(5)
    outer[...] = project(blocks, gbuf, 0)
    for i in range(6, len(copies)):
        wait(i)


def pack_kernel(a, b, d, packed):
    for i, ref in enumerate((a, b, d)):
        packed[i] = ref[...]


def near_kernel(packed, weights, wt, acc_in, sq_in, acc, sq, far, sem):
    blocks = [packed.at[i] for i in range(3)]
    wait = run_copies(weight_copies(wt, DRIVEN, other_masks()[2:], packed.shape[2], far, sem), 8)
    sq[...] = add_squares(sq_in[...], blocks)

    @pl.loop(0, 2)
    def _(k):
        acc[k] = acc_in[k] + project(blocks, weights, k)

    for i in range(2):
        wait(i)


def far_kernel(
    weights, packed, last_weights, wt, acc_in, sq_in, lam3, rowmask, scale, d3, e3, gate, both, sem
):
    _, rows, depth = packed.shape
    wait = run_copies(weight_copies(wt, GATE, own_masks()[1:] + other_masks()[:1], depth, gate, sem), 8)
    blocks = [packed.at[i] for i in range(3)]
    total = jnp.sum(add_squares(sq_in[...], blocks), axis=1, keepdims=True)
    row = lax.rsqrt(total / (8 * depth) + 1e-06)
    scale[...] = jnp.broadcast_to(row, scale.shape)

    @pl.loop(0, 2)
    def _(k):
        both[k] = acc_in[k] + project(blocks[:2], weights, k) + project(blocks[2:], last_weights, k)

    for g in range(SUB):
        cols = slice(g * LANE, (g + 1) * LANE)
        d3[:, g, :] = (both[0, :, cols] * scale[...]) * (both[1, :, cols] * scale[...])
    modes = lam3.shape[0]

    def body(step, state):
        first = pl.multiple_of(step * 32, 32)
        counts = rowmask[0, pl.ds(first, 32), :]
        for j in range(32):
            drive = d3[first + j] * counts[j : j + 1, :]
            state = [lam3[n] * state[n] + drive for n in range(modes)]
        return state

    zeros = [jnp.zeros((SUB, LANE), jnp.float32) for _ in range(modes)]
    state = lax.fori_loop(0, rows // 32, body, zeros)
    for n in range(modes):
        e3[n] = state[n]
    for i in range(3):
        wait(i)


def mark_rows(docs, rows, rowmask, valid):
    me = lax.axis_index("ctx")
    at = -me * rows
    first, last, starts = rows, -1, []
    for i in range(docs.shape[0]):
        inside = jnp.logical_and(at >= 0, at < rows)
        first = jnp.where(jnp.logical_and(inside, at < first), at, first)
        last = jnp.where(jnp.logical_and(inside, at > last), at, last)
        starts.append(at)
        at = at + docs[i]
    token = lax.broadcasted_iota(jnp.int32, rowmask.shape[1:], 0)
    rowmask[0] = jnp.where(token >= last, 1.0, 0.0)
    keep = jnp.ones(rowmask.shape[1:], jnp.float32)
    for at in starts:
        keep = jnp.where(token == at, 0.0, keep)
    rowmask[1] = keep
    rowmask[2] = jnp.where(token < first, 1.0, 0.0)
    reached = me >= 1
    for k in range(valid.shape[0]):
        if k > 0:
            for at in starts:
                between = jnp.logical_and(at >= -k * rows, at < -(k - 1) * rows)
                reached = jnp.logical_and(reached, jnp.logical_not(between))
            reached = jnp.logical_and(reached, me >= k + 1)
        valid[k] = jnp.full(valid.shape[1:], jnp.where(reached, 1.0, 0.0))


def outer_kernel(
    own, others, wt, sum_in, gate_far, d3, lam3, mix3, skip, rowmask, outer, f3, wbuf, sem
):
    _, rows, depth = own.shape
    a, b, d = [own.at[i] for i in range(3)]
    ao, bo, do = [others.at[i] for i in range(3)]
    modes = lam3.shape[0]
    wait = run_copies(weight_copies(wt, GATE, own_masks()[:1] + other_masks()[1:], depth, wbuf, sem), 8)

    def body(step, state):
        first = pl.multiple_of(step * 32, 32)
        keeps = rowmask[1, pl.ds(first, 32), :]
        for j in range(32):
            drive = d3[first + j]
            state = [lam3[n] * (state[n] * keeps[j : j + 1, :]) + drive for n in range(modes)]
            terms = [mix3[n] * state[n] for n in range(modes)]
            while len(terms) > 1:
                terms = [p + q for p, q in zip(terms[::2], terms[1::2])]
            f3[first + j] = terms[0] + skip[...] * drive
        return state

    zeros = [jnp.zeros((SUB, LANE), jnp.float32) for _ in range(modes)]
    lax.fori_loop(0, rows // 32, body, zeros)
    total = sum_in[...] + project((b, d, ao), gate_far, 0)
    for i, block in enumerate((a, bo, do)):
        wait(i)
        total = total + dot(block[...], wbuf[0, i * depth : (i + 1) * depth])
    outer[...] = total


def last_kernel(*refs, count):
    arrived = refs[:count]
    outer, f3, scale, lam3, mix3, rowmask, valid, out, buf, sem = refs[count:]
    rows = outer.shape[0]
    modes = lam3.shape[0]
    @pl.when(lax.axis_index("ctx") > 0)
    def _():
        state = []
        for n in range(modes):
            lam = lam3[n]
            whole = lam
            for _ in range(rows.bit_length() - 1):
                whole = whole * whole
            power, total = valid[0], jnp.zeros((SUB, LANE), jnp.float32)
            for k in range(count):
                total = total + power * arrived[k][n].astype(jnp.float32)
                if k + 1 < count:
                    power = valid[k + 1] * whole if k == 0 else valid[k + 1] * (power * whole)
            state.append(mix3[n] * total)

        def body(step, state):
            first = pl.multiple_of(step * 32, 32)
            reached = rowmask[2, pl.ds(first, 32), :]
            for j in range(32):
                t = first + j
                state = [lam3[n] * state[n] for n in range(modes)]
                terms = list(state)
                while len(terms) > 1:
                    terms = [a + b for a, b in zip(terms[::2], terms[1::2])]
                f3[t] = f3[t] + terms[0] * reached[j : j + 1, :]
            return state

        lax.fori_loop(0, rows // 32, body, state)

    copies = []
    for r in range(0, rows, PIECE):
        piece = slice(r, r + PIECE)
        for g in range(SUB):
            cols = slice(g * LANE, (g + 1) * LANE)
            buf[piece, cols] = (outer[piece, cols] * scale[piece] * f3[piece, g, :]).astype(buf.dtype)
        copies.append(pltpu.make_async_copy(buf.at[piece], out.at[piece], sem.at[r // PIECE]))
        copies[-1].start()
    for c in copies:
        c.wait()


def params(mib):
    return pltpu.CompilerParams(vmem_limit_bytes=mib << 20)


def fitted(stream, in_weight, pole_rate, residue, skip_gain, doc_lengths, reach):
    rows, depth = stream.shape
    width, _, local = in_weight.shape
    modes = pole_rate.shape[1]
    size = lax.axis_size("ch")
    wt = jnp.transpose(in_weight, (1, 0, 2))
    rate, res = pole_rate.T, residue.T
    f32, b16 = jnp.float32, jnp.bfloat16
    dma = pltpu.SemaphoreType.DMA

    def swap(block, mask):
        return lax.ppermute(block, "ch", [(i, i ^ mask) for i in range(size)])

    def split(block, first):
        masks = (4, 2) if first else (2, 4)
        return lax.ppermute(block, "ch", [(i, i ^ masks[i & 1]) for i in range(size)])

    def call(kernel, ins, outs, scratch, flops, mib):
        return pl.pallas_call(
            kernel,
            in_specs=[spec for spec, _ in ins],
            out_specs=[IN_VMEM] * len(outs),
            out_shape=outs,
            scratch_shapes=scratch,
            compiler_params=params(mib),
            cost_estimate=pl.CostEstimate(
                flops=2 * rows * depth * local * flops, bytes_accessed=0, transcendentals=0
            ),
            name=kernel.__name__,
        )(*[array for _, array in ins])

    def here(*arrays):
        return [(IN_VMEM, a) for a in arrays]

    planes = pltpu.VMEM((2, rows, local), f32)
    product = pltpu.VMEM((rows, local), f32)
    squares = pltpu.VMEM((rows, LANE), f32)
    poles = pltpu.VMEM((modes, SUB, LANE), f32)
    tokens = pltpu.VMEM((rows, SUB, LANE), f32)
    chunk = pltpu.VMEM((rows, depth), b16)
    vector = pltpu.VMEM((modes, local), f32)

    def there(*arrays):
        return [(IN_HBM, pltpu.with_memory_space_constraint(a, pltpu.HBM)) for a in arrays]

    def weights(planes_of, chunks):
        return pltpu.VMEM((planes_of, chunks * depth, local), b16)

    s = swap(stream, 1)
    a, b, d = split(stream, True), split(stream, False), swap(stream, 6)
    acc, outer, sq, lam3, mix3, near, far, rowmask, valid = call(
        first_kernel,
        there(stream) + here(s) + there(wt, rate, res, doc_lengths),
        [planes, product, squares, poles, poles, weights(2, 3), weights(2, 2)]
        + [pltpu.VMEM((3, rows, LANE), f32), pltpu.VMEM((reach, SUB, LANE), f32)],
        [chunk, weights(2, 2), weights(1, 2), vector, vector, pltpu.SMEM(doc_lengths.shape, jnp.int32), dma((16,)), dma((4,))],
        4,
        16,
    )
    a, b, d, acc, sq = lax.optimization_barrier((a, b, d, acc, sq))
    (own,) = call(pack_kernel, here(a, b, d), [pltpu.VMEM((3, rows, depth), b16)], [], 1, 1)
    others = swap(own, 1)
    acc, sq, far_d = call(
        near_kernel,
        here(own, near) + there(wt) + here(acc, sq),
        [planes, squares, weights(2, 1)],
        [dma((2,))],
        6,
        4,
    )
    scale, d3, e3, gate_far = call(
        far_kernel,
        here(far, others, far_d) + there(wt) + here(acc, sq, lam3, rowmask),
        [squares, tokens, poles, weights(1, 3)],
        [planes, dma((3,))],
        6,
        4,
    )
    ring = lax.axis_size("ctx")
    arrived = [
        lax.ppermute(e3 if k == 1 else e3.astype(b16), "ctx", [(i, (i + k) % ring) for i in range(ring)])
        for k in range(1, reach + 1)
    ]
    outer, f3 = call(
        outer_kernel,
        here(own, others)
        + there(wt)
        + here(outer, gate_far, d3, lam3, mix3, skip_gain.reshape(SUB, LANE), rowmask),
        [product, tokens],
        [weights(1, 3), dma((3,))],
        6,
        16,
    )
    return pl.pallas_call(
        functools.partial(last_kernel, count=reach),
        in_specs=[IN_VMEM] * (reach + 7),
        out_specs=IN_HBM,
        out_shape=jax.ShapeDtypeStruct((rows, local), b16),
        scratch_shapes=[chunk, dma((rows // PIECE,))],
        compiler_params=params(8),
        name="last",
    )(*arrived, outer, f3, scale, lam3, mix3, rowmask, valid)


def solution(mesh):
    placed = (P("ctx", "ch"), P(None, None, "ch"), P("ch", None), P("ch", None), P("ch"), P())
    ring = mesh.shape["ctx"]

    def per_device(*args):
        stream, in_weight = args[0], args[1]
        rows, depth = stream.shape
        longest = rows * ring // 2
        reach = min(ring - 1, (longest + rows - 2) // rows)
        if mesh.shape["ch"] == 8 and in_weight.shape[2] == SUB * LANE and rows == LANE:
            return fitted(*args, reach)
        return general(*args)

    return jax.shard_map(
        per_device, mesh=mesh, in_specs=placed, out_specs=P("ctx", "ch"), check_vma=False
    )
```

```python
import functools

import jax
import jax.numpy as jnp
from jax import lax
from jax.experimental import pallas as pl
from jax.experimental.pallas import tpu as pltpu
from jax.sharding import PartitionSpec as P

SUB = 8
LANE = 128
PIECE = 32
IN_VMEM = pl.BlockSpec(memory_space=pltpu.VMEM)
IN_HBM = pl.BlockSpec(memory_space=pltpu.HBM)
DRIVEN = (1, 2)
GATE = (0,)


def shifted(block, axis, distance):
    devices = range(lax.axis_size(axis))
    route = [(i - distance, i) for i in devices if i - distance in devices]
    return lax.ppermute(block, axis, route)


def combine(earlier, later):
    return (earlier[0] * later[0], later[0] * earlier[1] + later[1])


def split_proj(product, squares, width, local):
    rowscale = lax.rsqrt(squares / width + 1e-06)
    proj = product * rowscale[:, None]
    outer = proj[:, :local]
    driven = proj[:, local : 2 * local] * proj[:, 2 * local :]
    return (outer, driven)


def local_scan(driven, keep, lam):
    modes, local = lam.shape
    decay = keep[:, None, None] * lam[None, :, :]
    drive = jnp.broadcast_to(driven[:, None, :], (driven.shape[0], modes, local))
    return lax.associative_scan(combine, (decay, drive), axis=0)


def general(stream, in_weight, pole_rate, residue, skip_gain, doc_lengths):
    rows = stream.shape[0]
    width = in_weight.shape[0]
    local = in_weight.shape[2]
    modes = pole_rate.shape[1]
    weights = in_weight.reshape(width, 3 * local)
    lam = jnp.exp(-pole_rate).T
    mix = (residue * jnp.sqrt(-jnp.expm1(-2.0 * pole_rate))).T
    starts = jnp.cumsum(doc_lengths) - doc_lengths
    position = lax.axis_index("ctx") * rows + jnp.arange(rows, dtype=jnp.int32)
    is_start = jnp.any(position[:, None] == starts[None, :], axis=1)
    keep = jnp.where(is_start, 0.0, 1.0).astype(jnp.float32)
    whole = lax.all_gather(stream, "ch", axis=1, tiled=True)
    floats = whole.astype(jnp.float32)
    squares = jnp.sum(floats * floats, axis=1)
    product = jnp.dot(whole, weights, preferred_element_type=jnp.float32)
    outer, driven = split_proj(product, squares, width, local)
    decay_cum, local_state = local_scan(driven, keep, lam)
    block_decay = decay_cum[-1]
    block_state = local_state[-1]
    zeros_state = jnp.zeros((modes, local), jnp.float32)

    def forward(step, incoming):
        outgoing = block_decay * incoming + block_state
        return shifted(outgoing, "ctx", 1)

    incoming = lax.fori_loop(0, lax.axis_size("ctx") - 1, forward, zeros_state)
    state = local_state + decay_cum * incoming[None, :, :]
    filtered = jnp.einsum("tnc,nc->tc", state, mix)
    return (outer * (filtered + skip_gain[None, :] * driven)).astype(jnp.bfloat16)


def chunk_rows(mask, depth):
    return pl.ds(pl.multiple_of((lax.axis_index("ch") ^ mask) * depth, depth), depth)


def add_squares(sq, blocks):
    total = sq
    for ref in blocks:
        for g in range(ref.shape[1] // LANE):
            v = ref[:, g * LANE : (g + 1) * LANE].astype(jnp.float32)
            total = total + v * v
    return total


def by_groups(value, store):
    for g in range(SUB):
        store(g, value[:, g * LANE : (g + 1) * LANE])


def dot(a, b):
    return jnp.dot(a, b, preferred_element_type=jnp.float32)


def run_copies(copies, ahead):
    for c in copies[:ahead]:
        c.start()

    def wait(i):
        copies[i].wait()
        if i + ahead < len(copies):
            copies[i + ahead].start()

    return wait


def weight_copies(wt, planes, masks, depth, target, sem, at=0):
    return [
        pltpu.make_async_copy(
            wt.at[p, chunk_rows(m, depth)],
            target.at[k, pl.ds(i * depth, depth)],
            sem.at[at + k * len(masks) + i],
        )
        for k, p in enumerate(planes)
        for i, m in enumerate(masks)
    ]


def project(blocks, weights, plane):
    depth = blocks[0].shape[1]
    total = dot(blocks[0][...], weights[plane, :depth])
    for i in range(1, len(blocks)):
        total = total + dot(blocks[i][...], weights[plane, i * depth : (i + 1) * depth])
    return total


def own_masks():
    core = lax.axis_index("ch") & 1
    one, two = 4 - 2 * core, 2 + 2 * core
    return (one, two, 6)


def other_masks():
    core = lax.axis_index("ch") & 1
    one, two = 4 - 2 * core, 2 + 2 * core
    return (two ^ 1, one ^ 1, 7)


def first_kernel(
    o, s, wt, rate, res, lengths, acc, outer, sq, lam3, mix3, near, far, rowmask, valid, begins, held, wbuf, gbuf, rates, ress, docs, sem, small
):
    rows, depth = s.shape
    own = [
        pltpu.make_async_copy(o, held, small.at[0]),
        pltpu.make_async_copy(rate, rates, small.at[1]),
        pltpu.make_async_copy(res, ress, small.at[2]),
        pltpu.make_async_copy(lengths, docs, small.at[3]),
    ]
    copies = weight_copies(wt, DRIVEN, (0, 1), depth, wbuf, sem)
    copies += weight_copies(wt, GATE, (0, 1), depth, gbuf, sem, 4)
    copies += weight_copies(wt, DRIVEN, own_masks(), depth, near, sem, 6)
    copies += weight_copies(wt, DRIVEN, other_masks()[:2], depth, far, sem, 12)
    run_copies(own, len(own))
    wait = run_copies(copies, 6)
    for c in own:
        c.wait()
    blocks = (held, s)
    sq[...] = add_squares(jnp.zeros(sq.shape, jnp.float32), blocks)
    r = rates[...]
    lam = jnp.exp(-r)
    tanh = jnp.tanh(r)
    mix = ress[...] * jnp.sqrt(2.0 * tanh / (1.0 + tanh))

    def put_lam(g, v):
        lam3[:, g, :] = v

    def put_mix(g, v):
        mix3[:, g, :] = v

    by_groups(lam, put_lam)
    by_groups(mix, put_mix)
    mark_rows(docs, rows, rowmask, valid, begins)
    for k in range(2):
        wait(2 * k)
        wait(2 * k + 1)
        acc[k] = project(blocks, wbuf, k)
    wait(4)
    wait(5)
    outer[...] = project(blocks, gbuf, 0)
    for i in range(6, len(copies)):
        wait(i)


def pack_kernel(a, b, d, packed):
    for i, ref in enumerate((a, b, d)):
        packed[i] = ref[...]


def near_kernel(packed, weights, wt, acc_in, sq_in, acc, sq, far, sem):
    blocks = [packed.at[i] for i in range(3)]
    wait = run_copies(weight_copies(wt, DRIVEN, other_masks()[2:], packed.shape[2], far, sem), 8)
    sq[...] = add_squares(sq_in[...], blocks)

    @pl.loop(0, 2)
    def _(k):
        acc[k] = acc_in[k] + project(blocks, weights, k)

    for i in range(2):
        wait(i)


def far_kernel(
    weights, packed, last_weights, wt, acc_in, sq_in, lam3, rowmask, scale, d3, e3, gate, both, sem
):
    _, rows, depth = packed.shape
    wait = run_copies(weight_copies(wt, GATE, own_masks()[1:] + other_masks()[:1], depth, gate, sem), 8)
    blocks = [packed.at[i] for i in range(3)]
    total = jnp.sum(add_squares(sq_in[...], blocks), axis=1, keepdims=True)
    row = lax.rsqrt(total / (8 * depth) + 1e-06)
    scale[...] = jnp.broadcast_to(row, scale.shape)

    @pl.loop(0, 2)
    def _(k):
        both[k] = acc_in[k] + project(blocks[:2], weights, k) + project(blocks[2:], last_weights, k)

    for g in range(SUB):
        cols = slice(g * LANE, (g + 1) * LANE)
        d3[:, g, :] = (both[0, :, cols] * scale[...]) * (both[1, :, cols] * scale[...])
    modes = lam3.shape[0]

    def body(step, state):
        first = pl.multiple_of(step * 32, 32)
        counts = rowmask[0, pl.ds(first, 32), :]
        for j in range(32):
            drive = d3[first + j] * counts[j : j + 1, :]
            state = [lam3[n] * state[n] + drive for n in range(modes)]
        return state

    zeros = [jnp.zeros((SUB, LANE), jnp.float32) for _ in range(modes)]
    state = lax.fori_loop(0, rows // 32, body, zeros)
    for n in range(modes):
        e3[n] = state[n]
    for i in range(3):
        wait(i)


def mark_rows(docs, rows, rowmask, valid, begins):
    me = lax.axis_index("ctx")
    at = -me * rows
    first, last, starts = rows, -1, []
    for i in range(docs.shape[0]):
        inside = jnp.logical_and(at >= 0, at < rows)
        first = jnp.where(jnp.logical_and(inside, at < first), at, first)
        last = jnp.where(jnp.logical_and(inside, at > last), at, last)
        starts.append(at)
        at = at + docs[i]
    span = rows // begins.shape[0]
    for g in range(begins.shape[0]):
        begins[g] = jnp.int32(0)
        for at in starts:
            inside = jnp.logical_and(at >= g * span, at < (g + 1) * span)
            begins[g] = jnp.where(inside, 1, begins[g])
    token = lax.broadcasted_iota(jnp.int32, rowmask.shape[1:], 0)
    rowmask[0] = jnp.where(token >= last, 1.0, 0.0)
    keep = jnp.ones(rowmask.shape[1:], jnp.float32)
    for at in starts:
        keep = jnp.where(token == at, 0.0, keep)
    rowmask[1] = keep
    rowmask[2] = jnp.where(token < first, 1.0, 0.0)
    reached = me >= 1
    for k in range(valid.shape[0]):
        if k > 0:
            for at in starts:
                between = jnp.logical_and(at >= -k * rows, at < -(k - 1) * rows)
                reached = jnp.logical_and(reached, jnp.logical_not(between))
            reached = jnp.logical_and(reached, me >= k + 1)
        valid[k] = jnp.full(valid.shape[1:], jnp.where(reached, 1.0, 0.0))


def outer_kernel(
    own, others, wt, sum_in, gate_far, d3, lam3, mix3, skip, rowmask, begins, outer, f3, wbuf, sem
):
    _, rows, depth = own.shape
    a, b, d = [own.at[i] for i in range(3)]
    ao, bo, do = [others.at[i] for i in range(3)]
    modes = lam3.shape[0]
    wait = run_copies(weight_copies(wt, GATE, own_masks()[:1] + other_masks()[1:], depth, wbuf, sem), 8)

    def tokens(step, state, resets):
        first = pl.multiple_of(step * 32, 32)
        keeps = rowmask[1, pl.ds(first, 32), :]
        for j in range(32):
            drive = d3[first + j]
            if resets:
                state = [s * keeps[j : j + 1, :] for s in state]
            state = [lam3[n] * state[n] + drive for n in range(modes)]
            terms = [mix3[n] * state[n] for n in range(modes)]
            while len(terms) > 1:
                terms = [p + q for p, q in zip(terms[::2], terms[1::2])]
            f3[first + j] = terms[0] + skip[...] * drive
        return tuple(state)

    def body(step, state):
        return lax.cond(
            begins[step] > 0, lambda s: tokens(step, s, True), lambda s: tokens(step, s, False), state
        )

    zeros = tuple(jnp.zeros((SUB, LANE), jnp.float32) for _ in range(modes))
    lax.fori_loop(0, rows // 32, body, zeros)
    total = sum_in[...] + project((b, d, ao), gate_far, 0)
    for i, block in enumerate((a, bo, do)):
        wait(i)
        total = total + dot(block[...], wbuf[0, i * depth : (i + 1) * depth])
    outer[...] = total


def last_kernel(*refs, count):
    arrived = refs[:count]
    outer, f3, scale, lam3, mix3, rowmask, valid, out, buf, sem = refs[count:]
    rows = outer.shape[0]
    modes = lam3.shape[0]
    @pl.when(lax.axis_index("ctx") > 0)
    def _():
        state = []
        for n in range(modes):
            lam = lam3[n]
            whole = lam
            for _ in range(rows.bit_length() - 1):
                whole = whole * whole
            power, total = valid[0], jnp.zeros((SUB, LANE), jnp.float32)
            for k in range(count):
                total = total + power * arrived[k][n].astype(jnp.float32)
                if k + 1 < count:
                    power = valid[k + 1] * whole if k == 0 else valid[k + 1] * (power * whole)
            state.append(mix3[n] * total)

        def body(step, state):
            first = pl.multiple_of(step * 32, 32)
            reached = rowmask[2, pl.ds(first, 32), :]
            for j in range(32):
                t = first + j
                state = [lam3[n] * state[n] for n in range(modes)]
                terms = list(state)
                while len(terms) > 1:
                    terms = [a + b for a, b in zip(terms[::2], terms[1::2])]
                f3[t] = f3[t] + terms[0] * reached[j : j + 1, :]
            return state

        lax.fori_loop(0, rows // 32, body, state)

    copies = []
    for r in range(0, rows, PIECE):
        piece = slice(r, r + PIECE)
        for g in range(SUB):
            cols = slice(g * LANE, (g + 1) * LANE)
            buf[piece, cols] = (outer[piece, cols] * scale[piece] * f3[piece, g, :]).astype(buf.dtype)
        copies.append(pltpu.make_async_copy(buf.at[piece], out.at[piece], sem.at[r // PIECE]))
        copies[-1].start()
    for c in copies:
        c.wait()


def params(mib):
    return pltpu.CompilerParams(vmem_limit_bytes=mib << 20)


def fitted(stream, in_weight, pole_rate, residue, skip_gain, doc_lengths, reach):
    rows, depth = stream.shape
    width, _, local = in_weight.shape
    modes = pole_rate.shape[1]
    size = lax.axis_size("ch")
    wt = jnp.transpose(in_weight, (1, 0, 2))
    rate, res = pole_rate.T, residue.T
    f32, b16 = jnp.float32, jnp.bfloat16
    dma = pltpu.SemaphoreType.DMA

    def swap(block, mask):
        return lax.ppermute(block, "ch", [(i, i ^ mask) for i in range(size)])

    def split(block, first):
        masks = (4, 2) if first else (2, 4)
        return lax.ppermute(block, "ch", [(i, i ^ masks[i & 1]) for i in range(size)])

    def call(kernel, ins, outs, scratch, flops, mib):
        return pl.pallas_call(
            kernel,
            in_specs=[spec for spec, _ in ins],
            out_specs=[pl.BlockSpec(memory_space=o.memory_space) for o in outs],
            out_shape=outs,
            scratch_shapes=scratch,
            compiler_params=params(mib),
            cost_estimate=pl.CostEstimate(
                flops=2 * rows * depth * local * flops, bytes_accessed=0, transcendentals=0
            ),
            name=kernel.__name__,
        )(*[array for _, array in ins])

    def here(*arrays):
        return [(IN_VMEM, a) for a in arrays]

    planes = pltpu.VMEM((2, rows, local), f32)
    product = pltpu.VMEM((rows, local), f32)
    squares = pltpu.VMEM((rows, LANE), f32)
    poles = pltpu.VMEM((modes, SUB, LANE), f32)
    tokens = pltpu.VMEM((rows, SUB, LANE), f32)
    chunk = pltpu.VMEM((rows, depth), b16)
    vector = pltpu.VMEM((modes, local), f32)

    def there(*arrays):
        return [(IN_HBM, pltpu.with_memory_space_constraint(a, pltpu.HBM)) for a in arrays]

    def weights(planes_of, chunks):
        return pltpu.VMEM((planes_of, chunks * depth, local), b16)

    s = swap(stream, 1)
    a, b, d = split(stream, True), split(stream, False), swap(stream, 6)
    acc, outer, sq, lam3, mix3, near, far, rowmask, valid, begins = call(
        first_kernel,
        there(stream) + here(s) + there(wt, rate, res, doc_lengths),
        [planes, product, squares, poles, poles, weights(2, 3), weights(2, 2)]
        + [pltpu.VMEM((3, rows, LANE), f32), pltpu.VMEM((reach, SUB, LANE), f32)]
        + [pltpu.SMEM((rows // 32,), jnp.int32)],
        [chunk, weights(2, 2), weights(1, 2), vector, vector, pltpu.SMEM(doc_lengths.shape, jnp.int32), dma((16,)), dma((4,))],
        4,
        16,
    )
    a, b, d, acc, sq = lax.optimization_barrier((a, b, d, acc, sq))
    (own,) = call(pack_kernel, here(a, b, d), [pltpu.VMEM((3, rows, depth), b16)], [], 1, 1)
    others = swap(own, 1)
    acc, sq, far_d = call(
        near_kernel,
        here(own, near) + there(wt) + here(acc, sq),
        [planes, squares, weights(2, 1)],
        [dma((2,))],
        6,
        4,
    )
    scale, d3, e3, gate_far = call(
        far_kernel,
        here(far, others, far_d) + there(wt) + here(acc, sq, lam3, rowmask),
        [squares, tokens, poles, weights(1, 3)],
        [planes, dma((3,))],
        6,
        4,
    )
    ring = lax.axis_size("ctx")
    arrived = [
        lax.ppermute(e3 if k == 1 else e3.astype(b16), "ctx", [(i, (i + k) % ring) for i in range(ring)])
        for k in range(1, reach + 1)
    ]
    outer, f3 = call(
        outer_kernel,
        here(own, others)
        + there(wt)
        + here(outer, gate_far, d3, lam3, mix3, skip_gain.reshape(SUB, LANE), rowmask)
        + [(pl.BlockSpec(memory_space=pltpu.SMEM), begins)],
        [product, tokens],
        [weights(1, 3), dma((3,))],
        6,
        16,
    )
    return pl.pallas_call(
        functools.partial(last_kernel, count=reach),
        in_specs=[IN_VMEM] * (reach + 7),
        out_specs=IN_HBM,
        out_shape=jax.ShapeDtypeStruct((rows, local), b16),
        scratch_shapes=[chunk, dma((rows // PIECE,))],
        compiler_params=params(8),
        name="last",
    )(*arrived, outer, f3, scale, lam3, mix3, rowmask, valid)


def solution(mesh):
    placed = (P("ctx", "ch"), P(None, None, "ch"), P("ch", None), P("ch", None), P("ch"), P())
    ring = mesh.shape["ctx"]

    def per_device(*args):
        stream, in_weight = args[0], args[1]
        rows, depth = stream.shape
        longest = rows * ring // 2
        reach = min(ring - 1, (longest + rows - 2) // rows)
        if mesh.shape["ch"] == 8 and in_weight.shape[2] == SUB * LANE and rows == LANE:
            return fitted(*args, reach)
        return general(*args)

    return jax.shard_map(
        per_device, mesh=mesh, in_specs=placed, out_specs=P("ctx", "ch"), check_vma=False
    )
```
